256 devices in a mesh: dp: 32 (over y, x, core), tensor: 8 (over z).
Axes of the slice: x: 4, y: 4, z: 8, core: 2. Of those that a mesh axis runs over, the one named last changes fastest.
Arguments:
- inputs: bfloat16 [8192, 4096], P('dp', 'tensor'), may hold values from -6 to 6
- weight: bfloat16 [4096, 4096], P('tensor'), may hold values from -0.046875 to 0.046875
- out_grad: bfloat16 [8192, 4096], P(('dp', 'tensor')), may hold values from -0.25 to 0.25
- error_feedback: bfloat16 [32, 4096, 4096], P('dp', 'tensor'), may hold values from -4 to 4
- warm_coeffs: float32 [8, 8, 4096], P('tensor'), may hold values from -6 to 6
Outputs:
- outputs: bfloat16 [8192, 4096], P(('dp', 'tensor'))
- new_basis: float32 [8, 4096], P(None, 'tensor')
- new_coeffs: float32 [8, 8, 4096], P('tensor')
- new_error: bfloat16 [32, 4096, 4096], P('dp', 'tensor')
The draws below stay inside these ranges and needn't reach their ends.
All inputs are finite; a program needn't handle non-finite values.
Results may differ from the reference program's by a relative error of at most 0.001.
Values may be sent and summed in bfloat16 or wider, within the bound.
A program may use at most 128 MiB of HBM per device.

```python
import math
import jax
import jax.numpy as jnp
from jax import lax

ROWS = 4096
COLS = 4096
RANK = 8
TOK = 256
REPLICAS = 32
BLOCKS = 8
SHARD = 512
TOKENS = 8192


def shard_levels(own_key, dims, cuts, least, high):
    gain, own = 1.0, jax.random.fold_in(own_key, 6)
    for axis_at, parts in cuts:
        steps = jnp.exp(jax.random.uniform(jax.random.fold_in(own, axis_at), (parts,), jnp.float32, least / len(cuts), high / len(cuts)))
        gain = gain * jnp.repeat(steps, dims[axis_at] // parts).reshape([-1 if axis == axis_at else 1 for axis in range(len(dims))])
    return gain


def bell_draw(own_key, dims, spread, bound, pieces=(), held_as=jnp.bfloat16):
    array = jax.random.normal(own_key, dims, jnp.float32) * spread
    if len(pieces) > 0:
        array = shard_levels(own_key, dims, pieces, -0.22, 0.18) * array
    return jnp.clip(array, min=-bound, max=bound).astype(held_as)


def setup_inputs(seed: int = 0) -> dict:
    splits = jax.random.split(jax.random.key(seed), 6)
    inputs = bell_draw(splits[0], (TOKENS, ROWS), 1.0, 6.0, ((0, 32), (1, 8)))
    weight = bell_draw(splits[1], (ROWS, COLS), (4 * ROWS) ** -0.5, 0.046875, ((0, 8),))
    out_grad = bell_draw(splits[2], (TOKENS, COLS), 0.015625, 0.25, ((0, 256),))
    error_feedback = bell_draw(splits[3], (REPLICAS, ROWS, COLS), 0.25, 4.0, ((0, 32), (1, 8)))
    warm_coeffs = bell_draw(splits[4], (BLOCKS, RANK, COLS), 1.0, 6.0, ((0, 8),), jnp.float32)
    return dict(inputs=inputs, weight=weight, out_grad=out_grad, error_feedback=error_feedback, warm_coeffs=warm_coeffs)


exact_precision = lax.Precision.HIGHEST
epsilon = 1e-06

def orthonormal(sketch_rows):
    kept_rows = []
    for row_index in range(sketch_rows.shape[0]):
        vector = sketch_rows[row_index]
        for earlier in kept_rows:
            vector = vector - jnp.sum(vector * earlier) * earlier
        vector = vector * lax.rsqrt(jnp.sum(vector * vector) + epsilon)
        kept_rows.append(vector)
    return jnp.stack(kept_rows)

def replica_matrix(inputs, out_grad, error_feedback, replica):
    first_row = (replica * TOK).astype(jnp.int32)
    left_rows = lax.dynamic_slice_in_dim(inputs, first_row, TOK, 0)
    right_rows = lax.dynamic_slice_in_dim(out_grad, first_row, TOK, 0)
    gradient = jnp.dot(left_rows.T, right_rows, preferred_element_type=jnp.float32)
    own_error = lax.dynamic_index_in_dim(error_feedback, replica, 0, keepdims=False)
    return (own_error.astype(jnp.float32) + gradient).reshape(BLOCKS, SHARD, COLS)

def reference(inputs, weight, out_grad, error_feedback, warm_coeffs):
    outputs = jnp.dot(inputs, weight, preferred_element_type=jnp.float32).astype(jnp.bfloat16)
    replicas = jnp.arange(REPLICAS, dtype=jnp.int32)

    def add_sketch(running, replica):
        merged = replica_matrix(inputs, out_grad, error_feedback, replica)
        return (running + jnp.einsum('trc,tdc->trd', warm_coeffs, merged, precision=exact_precision), None)
    sketch, _ = lax.scan(add_sketch, jnp.zeros((BLOCKS, RANK, SHARD), jnp.float32), replicas)
    unit_rows = jax.vmap(orthonormal)(sketch)

    def add_coeffs(running, replica):
        merged = replica_matrix(inputs, out_grad, error_feedback, replica)
        return (running + jnp.einsum('trd,tdc->trc', unit_rows, merged, precision=exact_precision), None)
    coeff_total, _ = lax.scan(add_coeffs, jnp.zeros((BLOCKS, RANK, COLS), jnp.float32), replicas)
    new_coeffs = coeff_total / REPLICAS

    def residual_of(replica):
        merged = replica_matrix(inputs, out_grad, error_feedback, replica)
        approx = jnp.einsum('trd,trc->tdc', unit_rows, new_coeffs, precision=exact_precision)
        return (merged - approx).reshape(ROWS, COLS).astype(jnp.bfloat16)
    new_error = lax.map(residual_of, replicas)
    new_basis = jnp.transpose(unit_rows, (1, 0, 2)).reshape(RANK, ROWS) * math.sqrt(SHARD)
    return (outputs, new_basis, new_coeffs, new_error)
```

```python
import functools
import math

import jax
import jax.numpy as jnp
from jax import lax
from jax.experimental import pallas as pl
from jax.experimental.pallas import tpu as pltpu
from jax.sharding import PartitionSpec as P

MESH = pl.DeviceIdType.MESH
F32 = jnp.float32
BF16 = jnp.bfloat16
EPSILON = 1e-06
TILE = 512
XS, YS, CORES = 4, 4, 2
PLANE = XS * CORES
DO_G, DO_RS, DO_AR = True, True, True


def nn(a, b):
    return lax.dot_general(a, b, (((1,), (0,)), ((), ())), preferred_element_type=F32)


def nt(a, b):
    return lax.dot_general(a, b, (((1,), (1,)), ((), ())), preferred_element_type=F32)


def pieces(v):
    high = v.astype(BF16).astype(F32)
    rest = v - high
    middle = rest.astype(BF16).astype(F32)
    return high, middle, rest - middle


def split3(v):
    return jnp.concatenate(pieces(v), axis=0).astype(BF16)


def sum3(v):
    n = v.shape[0] // 3
    return v[:n] + v[n : 2 * n] + v[2 * n :]


def orthonormal(v):
    rows = lax.broadcasted_iota(jnp.int32, (v.shape[0], 1), 0)
    for i in range(v.shape[0]):
        row = v[i : i + 1]
        dots = jnp.sum(v * row, axis=1, keepdims=True)
        scale = lax.rsqrt(dots[i : i + 1] + EPSILON)
        unit = row * scale
        v = jnp.where(rows == i, unit, jnp.where(rows > i, v - (dots * scale) * unit, v))
    return v


def main_kernel(
    x_hbm, w_hbm, g_hbm, e_hbm, wc_ref,
    out_ref, basis_ref, coef_ref, g_out, lhs_ref, u_ref,
    x_ref, w_ref, e_ref, gbuf, part, rbuf, wc3_ref, se_ref, cbuf,
    abuf, bbuf, abuf2, bbuf2, sk_src,
    lsem, g_send, g_recv, rs_send, rs_recv, sk_send, sk_recv, cf_send, cf_recv,
):
    n = 8
    me = lax.axis_index("tensor")
    dp = lax.axis_index("dp")
    y, xc = dp // PLANE, dp % PLANE
    z_to = [lax.rem(me + 1, n), lax.rem(me + n - 1, n)]
    sign = (1, -1)
    a_to = [y * PLANE + lax.rem(xc + k, PLANE) for k in range(PLANE)]
    b_to = [lax.rem(y + k, YS) * PLANE + xc for k in range(YS)]

    lx = pltpu.make_async_copy(x_hbm, x_ref, lsem.at[0])
    lw = pltpu.make_async_copy(w_hbm, w_ref, lsem.at[1])
    le = pltpu.make_async_copy(e_hbm, e_ref, lsem.at[2])
    own = pl.ds(pl.multiple_of(me * 32, 32), 32)
    lg = pltpu.make_async_copy(g_hbm, gbuf.at[own], lsem.at[3])
    lg.start()
    lx.start()
    lw.start()
    le.start()

    barrier = pltpu.get_barrier_semaphore()
    for z in z_to:
        pl.semaphore_signal(barrier, inc=1, device_id={"tensor": z}, device_id_type=MESH)
    for d in a_to[1:] + b_to[1:]:
        pl.semaphore_signal(barrier, inc=1, device_id={"dp": d}, device_id_type=MESH)
    pl.semaphore_wait(barrier, 2 + (PLANE - 1) + (YS - 1))

    def steps(d, h):
        return 4 if d == h else 3

    def g_copy(d, h, s):
        block = lax.rem(me - sign[d] * s + n, n)
        at = pl.ds(pl.multiple_of(block * 32 + h * 16, 16), 16)
        return pltpu.make_async_remote_copy(
            src_ref=gbuf.at[at], dst_ref=gbuf.at[at],
            send_sem=g_send.at[d, h, s], recv_sem=g_recv.at[d, h, s],
            device_id={"tensor": z_to[d]}, device_id_type=MESH)

    def g_step(s):
        for h in range(2):
            for d in range(2):
                if s > 0 and s - 1 < steps(d, h):
                    g_copy(d, h, s - 1).wait_recv()
                if s < steps(d, h):
                    g_copy(d, h, s).start()

    def rs_copy(d, q, s):
        k = steps(d, q // 2)
        dest = lax.rem(me + sign[d] * (k - s) + n, n)
        at = pl.ds(pl.multiple_of(dest * 32, 32), 32)
        cols = pl.ds(q * 1024, 1024)
        return pltpu.make_async_remote_copy(
            src_ref=part.at[at, cols], dst_ref=rbuf.at[d, s, :, cols],
            send_sem=rs_send.at[d, q, s], recv_sem=rs_recv.at[d, q, s],
            device_id={"tensor": z_to[d]}, device_id_type=MESH)

    def rs_step(s, qs=range(4)):
        for q in qs:
            for d in range(2):
                k = steps(d, q // 2)
                cols = pl.ds(q * 1024, 1024)
                if s > 0 and s - 1 < k:
                    rs_copy(d, q, s - 1).wait_recv()
                    dest = lax.rem(me + sign[d] * (k - s) + n, n)
                    at = pl.ds(pl.multiple_of(dest * 32, 32), 32)
                    part[at, cols] += rbuf[d, s - 1, :, cols]
                if s < k:
                    rs_copy(d, q, s).start()

    lg.wait()
    if DO_G:
        g_step(0)
    lx.wait()
    lw.wait()

    @pl.loop(0, 4096, step=TILE)
    def _(c):
        cols = pl.ds(pl.multiple_of(c, TILE), TILE)
        part[:, cols] = nn(x_ref[...], w_ref[:, cols])

    if DO_G:
        g_step(1)
    le.wait()
    if DO_AR:
        wc3_ref[...] = split3(wc_ref[...])
        lhs_ref[...] = x_ref[...].T
        se_ref[...] = jnp.zeros_like(se_ref)

        @pl.loop(0, 4096, step=TILE)
        def _(c):
            cols = pl.ds(pl.multiple_of(c, TILE), TILE)
            se_ref[...] += nt(wc3_ref[:, cols], e_ref[:, cols])

    if DO_G:
        g_step(2)
        g_step(3)
    if DO_RS:
        rs_step(0)
    if DO_G:
        g_step(4)
    lgo = pltpu.make_async_copy(gbuf, g_out, lsem.at[4])
    lgo.start()

    if DO_AR:
        t3 = jnp.zeros((24, 256), F32)
        for c in range(0, 4096, TILE):
            t3 += nt(wc3_ref[:, c : c + TILE], gbuf[:, c : c + TILE])
        sketch = sum3(se_ref[...]) + sum3(nn(split3(sum3(t3)), x_ref[...]))

        def a_copy(k, src, dst, send, recv):
            return pltpu.make_async_remote_copy(
                src_ref=src, dst_ref=dst, send_sem=send.at[k], recv_sem=recv.at[k],
                device_id={"dp": a_to[k]}, device_id_type=MESH)

        def b_copy(k, src, dst, send, recv):
            return pltpu.make_async_remote_copy(
                src_ref=src, dst_ref=dst, send_sem=send.at[PLANE + k], recv_sem=recv.at[PLANE + k],
                device_id={"dp": b_to[k]}, device_id_type=MESH)

        ks_a, ks_b = range(1, PLANE), range(1, YS)
        sk_src[0] = sketch
        copies = [a_copy(k, sk_src.at[0], abuf.at[xc], sk_send, sk_recv) for k in ks_a]
        for c in copies:
            c.start()
        abuf[xc] = sketch
        for c in copies:
            c.wait_recv()
        total = abuf[0]
        for k in range(1, PLANE):
            total += abuf[k]
        sk_src[1] = total
        copies2 = [b_copy(k, sk_src.at[1], bbuf.at[y], sk_send, sk_recv) for k in ks_b]
        for c in copies2:
            c.start()
        bbuf[y] = total
        for c in copies2:
            c.wait_recv()
        total = bbuf[0]
        for k in range(1, YS):
            total += bbuf[k]
        for c in copies + copies2:
            c.wait_send()
        unit = orthonormal(total)
        basis_ref[...] = unit * math.sqrt(512)
        u_ref[...] = unit
        if DO_RS:
            rs_step(1, [0, 1])
        u3 = split3(unit)
        v3 = split3(sum3(nt(u3, x_ref[...])))

        def slab(j):
            return pl.ds(pl.multiple_of(j * 512, 512), 512)

        @pl.loop(0, 4096, step=TILE)
        def _(c):
            cols = pl.ds(pl.multiple_of(c, TILE), TILE)
            cbuf[:, cols] = sum3(nn(u3, e_ref[:, cols]) + nn(v3, gbuf[:, cols]))

        copies = [a_copy(k, cbuf.at[:, slab(lax.rem(xc + k, PLANE))], abuf2.at[xc], cf_send.at[0], cf_recv.at[0]) for k in ks_a]
        for c in copies:
            c.start()
        abuf2[xc] = cbuf[:, slab(xc)]
        for c in copies:
            c.wait_recv()
        total = abuf2[0]
        for k in range(1, PLANE):
            total += abuf2[k]
        for k in range(YS):
            sk_src[2, :, k * 128 : k * 128 + 128] = total[:, k * 128 : k * 128 + 128]

        def piece(j):
            return pl.ds(pl.multiple_of(j * 128, 128), 128)

        copies2 = [b_copy(k, sk_src.at[2, :, piece(lax.rem(y + k, YS))], bbuf2.at[y], cf_send.at[0], cf_recv.at[0]) for k in ks_b]
        for c in copies2:
            c.start()
        bbuf2[y] = sk_src[2, :, piece(y)]
        for c in copies2:
            c.wait_recv()
        if DO_RS:
            rs_step(1, [2, 3])
        for c in copies + copies2:
            c.wait_send()
        total = bbuf2[0]
        for k in range(1, YS):
            total += bbuf2[k]
        total = total * (1.0 / 32)
        mine = pl.ds(pl.multiple_of(xc * 512 + y * 128, 128), 128)
        coef_ref[:, mine] = total
        copies = [b_copy(k, coef_ref.at[:, mine], coef_ref.at[:, mine], cf_send.at[1], cf_recv.at[1]) for k in ks_b]
        for c in copies:
            c.start()
        for c in copies:
            c.wait_recv()
        copies2 = [a_copy(k, coef_ref.at[:, slab(xc)], coef_ref.at[:, slab(xc)], cf_send.at[1], cf_recv.at[1]) for k in ks_a]
        for c in copies2:
            c.start()
        for c in copies2:
            c.wait_recv()
        for c in copies + copies2:
            c.wait_send()
    elif DO_RS:
        rs_step(1)
    if DO_RS:
        rs_step(2)
        rs_step(3)
        rs_step(4)
    out_ref[...] = part[own, :].astype(BF16)
    if DO_G:
        for d in range(2):
            for h in range(2):
                for s in range(steps(d, h)):
                    g_copy(d, h, s).wait_send()
    if DO_RS:
        for d in range(2):
            for q in range(4):
                for s in range(steps(d, q // 2)):
                    rs_copy(d, q, s).wait_send()
    lgo.wait()


def error_kernel(x_ref, u_ref, c_ref, e_ref, g_ref, o_ref):
    c0, c1, c2 = pieces(c_ref[...])
    u0, u1, u2 = pieces(u_ref[...])
    right = jnp.concatenate([c0, c1, c0, c2, c0, c1], axis=0).astype(BF16)
    left = jnp.concatenate([u0, u0, u1, u0, u2, u1], axis=0).T.astype(BF16)
    low = nn(left, right)
    o_ref[...] = (e_ref[...].astype(F32) + nn(x_ref[...], g_ref[...]) - low).astype(BF16)


def shards(inputs, weight, out_grad, error_feedback, warm_coeffs):
    S = jax.ShapeDtypeStruct
    V = pl.BlockSpec(memory_space=pltpu.VMEM)
    A = pl.BlockSpec(memory_space=pl.ANY)
    D = pltpu.SemaphoreType.DMA
    out, basis, coef, g_all, xt, unit = pl.pallas_call(
        main_kernel,
        out_shape=(S((32, 4096), BF16), S((8, 512), F32), S((8, 4096), F32), S((256, 4096), BF16),
                   S((512, 256), BF16), S((8, 512), F32)),
        in_specs=[A, A, A, A, V],
        out_specs=(V, V, V, A, V, V),
        scratch_shapes=[
            pltpu.VMEM((256, 512), BF16),
            pltpu.VMEM((512, 4096), BF16),
            pltpu.VMEM((512, 4096), BF16),
            pltpu.VMEM((256, 4096), BF16),
            pltpu.VMEM((256, 4096), F32),
            pltpu.VMEM((2, 4, 32, 4096), F32),
            pltpu.VMEM((24, 4096), BF16),
            pltpu.VMEM((24, 512), F32),
            pltpu.VMEM((8, 4096), F32),
            pltpu.VMEM((PLANE, 8, 512), F32),
            pltpu.VMEM((YS, 8, 512), F32),
            pltpu.VMEM((PLANE, 8, 512), F32),
            pltpu.VMEM((YS, 8, 128), F32),
            pltpu.VMEM((3, 8, 512), F32),
            D((5,)),
            D((2, 2, 4)), D((2, 2, 4)),
            D((2, 4, 4)), D((2, 4, 4)),
            D((PLANE + YS,)), D((PLANE + YS,)),
            D((2, PLANE + YS)), D((2, PLANE + YS)),
        ],
        compiler_params=pltpu.CompilerParams(
            collective_id=0, has_side_effects=True, vmem_limit_bytes=48 * 2**20),
    )(inputs, weight, out_grad, error_feedback[0], warm_coeffs[0])
    whole = lambda i: (0, 0)
    cols = lambda i: (0, i)
    err = pl.pallas_call(
        error_kernel,
        grid=(4096 // TILE,),
        out_shape=S((512, 4096), BF16),
        in_specs=[pl.BlockSpec((512, 256), whole), pl.BlockSpec((8, 512), whole), pl.BlockSpec((8, TILE), cols),
                  pl.BlockSpec((512, TILE), cols), pl.BlockSpec((256, TILE), cols)],
        out_specs=pl.BlockSpec((512, TILE), cols),
        compiler_params=pltpu.CompilerParams(vmem_limit_bytes=24 * 2**20),
    )(xt, unit, coef, error_feedback[0], g_all)
    return (out, basis, coef[None], err[None])


def solution(mesh):
    in_specs = (
        P("dp", "tensor"),
        P("tensor", None),
        P(("dp", "tensor"), None),
        P("dp", "tensor", None),
        P("tensor", None, None),
    )
    out_specs = (
        P(("dp", "tensor"), None),
        P(None, "tensor"),
        P("tensor", None, None),
        P("dp", "tensor", None),
    )
    return jax.shard_map(shards, mesh=mesh, in_specs=in_specs, out_specs=out_specs, check_vma=False)
```

```python
import functools
import math

import jax
import jax.numpy as jnp
from jax import lax
from jax.experimental import pallas as pl
from jax.experimental.pallas import tpu as pltpu
from jax.sharding import PartitionSpec as P

MESH = pl.DeviceIdType.MESH
F32 = jnp.float32
BF16 = jnp.bfloat16
EPSILON = 1e-06
TILE = 512
PARTS = 4
XS, YS, CORES = 4, 4, 2
PLANE = XS * CORES
DP = YS * PLANE


def nn(a, b):
    return lax.dot_general(a, b, (((1,), (0,)), ((), ())), preferred_element_type=F32)


def nt(a, b):
    return lax.dot_general(a, b, (((1,), (1,)), ((), ())), preferred_element_type=F32)


def pieces(v):
    high = v.astype(BF16).astype(F32)
    rest = v - high
    middle = rest.astype(BF16).astype(F32)
    return high, middle, rest - middle


def split3(v):
    return jnp.concatenate(pieces(v), axis=0).astype(BF16)


def sum3(v):
    n = v.shape[0] // 3
    return v[:n] + v[n : 2 * n] + v[2 * n :]


def orthonormal(v):
    rows = lax.broadcasted_iota(jnp.int32, (v.shape[0], 1), 0)
    for i in range(v.shape[0]):
        row = v[i : i + 1]
        dots = jnp.sum(v * row, axis=1, keepdims=True)
        scale = lax.rsqrt(dots[i : i + 1] + EPSILON)
        unit = row * scale
        v = jnp.where(rows == i, unit, jnp.where(rows > i, v - (dots * scale) * unit, v))
    return v


def main_kernel(
    x_hbm, w_hbm, g_hbm, e_hbm, wc_hbm,
    out_ref, coef_ref, merged_ref, u_ref,
    x_ref, e_ref, gbuf, xa, wp, yacc, yb, wc_ref, wz, w3_ref, gpad, tsrc, tdst, se_ref, xt_ref, cbuf,
    abuf, bbuf, cin, sk_src,
    lsem, g_send, g_recv, xz_send, xz_recv, xy_send, xy_recv, w_send, w_recv, wc_send, wc_recv,
    y_send, y_recv, sk_send, sk_recv, cf_send, cf_recv, c_send, c_recv, p_send, p_recv, k_send, k_recv,
    t_send, t_recv,
):
    n = 8
    me = lax.axis_index("tensor")
    dp = lax.axis_index("dp")
    core = dp % CORES
    chip = dp // CORES
    y, xc = dp // PLANE, dp % PLANE
    xq = xc // CORES
    z_all = [lax.rem(me + k, n) for k in range(n)]
    z_to = [z_all[1], z_all[n - 1]]
    sign = (1, -1)
    a_to = [y * PLANE + lax.rem(xc + k, PLANE) for k in range(PLANE)]
    b_to = [lax.rem(y + k, YS) * PLANE + xc for k in range(YS)]
    d_to = [lax.rem(dp + k, DP) for k in range(DP)]
    chips = [lax.rem(chip + k, XS * YS) for k in range(XS * YS)]
    p_to = [c * CORES + core for c in chips]
    partner = chip * CORES + (1 - core)

    def shifted(axis, r):
        if axis == 0:
            return y * XS + lax.rem(xq + r + XS, XS)
        return lax.rem(y + r + YS, YS) * XS + xq

    own = pl.ds(pl.multiple_of(me * 32, 32), 32)
    mine = pl.ds(pl.multiple_of(chip * 32, 32), 32)
    own_cols = pl.ds(pl.multiple_of(me * 512, 512), 512)
    own_rows = own_cols
    chip_cols = pl.ds(pl.multiple_of(chip * 256, 256), 256)
    lx = pltpu.make_async_copy(x_hbm, x_ref, lsem.at[0])
    lw = pltpu.make_async_copy(w_hbm.at[:, chip_cols], wp.at[own_rows, :], lsem.at[1])
    le = pltpu.make_async_copy(e_hbm, e_ref, lsem.at[2])
    lg = pltpu.make_async_copy(g_hbm, gbuf.at[own], lsem.at[3])
    lc = pltpu.make_async_copy(wc_hbm, wc_ref, lsem.at[5])
    lp = pltpu.make_async_copy(g_hbm, gpad.at[pl.ds(pl.multiple_of(lax.rem(me, 4) * 32, 32), 32)], lsem.at[4])
    for c in (lc, lx, lg, le, lw):
        c.start()

    barrier = pltpu.get_barrier_semaphore()
    for z in z_all[1:]:
        pl.semaphore_signal(barrier, inc=1, device_id={"tensor": z}, device_id_type=MESH)
    for d in d_to[1:]:
        pl.semaphore_signal(barrier, inc=1, device_id={"dp": d}, device_id_type=MESH)
    gpad[...] = jnp.zeros_like(gpad)
    lp.start()
    pl.semaphore_wait(barrier, 7 + 31)

    def settle(ref, sem):
        pltpu.make_async_copy(ref, ref, sem).wait()

    def steps(d, h):
        return 4 if d == h else 3

    def ring_copy(buf, rows, part, cols, send, recv, d, h, s):
        block = lax.rem(me - sign[d] * s + n, n)
        at = pl.ds(pl.multiple_of(block * rows + h * part, part), part)
        return pltpu.make_async_remote_copy(
            src_ref=buf.at[at, cols], dst_ref=buf.at[at, cols],
            send_sem=send, recv_sem=recv.at[d, h, s],
            device_id={"tensor": z_to[d]}, device_id_type=MESH)

    def g_copy(d, h, s):
        return ring_copy(gbuf, 32, 16, slice(None), g_send, g_recv, d, h, s)

    core_cols = pl.ds(pl.multiple_of(core * 128, 128), 128)

    def w_copy(d, h, s):
        return ring_copy(wp, 512, 256, core_cols, w_send, w_recv, d, h, s)

    def wc_copy(d, h, s):
        block = lax.rem(me - sign[d] * (s + 1) + n, n)
        at = pl.ds(pl.multiple_of(block * 512 + h * 256, 256), 256)
        return pltpu.make_async_remote_copy(
            src_ref=wp.at[at, core_cols], dst_ref=wp.at[at, core_cols],
            send_sem=wc_send, recv_sem=wc_recv.at[s],
            device_id={"dp": partner}, device_id_type=MESH)

    def g_step(s):
        for h in range(2):
            for d in range(2):
                if s > 0 and s - 1 < steps(d, h):
                    g_copy(d, h, s - 1).wait_recv()
                if s < steps(d, h):
                    g_copy(d, h, s).start()

    def w_step(s):
        for h in range(2):
            for d in range(2):
                if s > 0 and s - 1 < steps(d, h):
                    w_copy(d, h, s - 1).wait_recv()
                if s < steps(d, h):
                    w_copy(d, h, s).start()
                if s > 0 and s - 1 < steps(d, h):
                    wc_copy(d, h, s - 1).start()

    def xz_copy(k):
        src = pl.ds(pl.multiple_of(z_all[k] * 32, 32), 32)
        return pltpu.make_async_remote_copy(
            src_ref=x_ref.at[src], dst_ref=xa.at[mine, own_cols],
            send_sem=xz_send, recv_sem=xz_recv,
            device_id={"tensor": z_all[k]}, device_id_type=MESH)

    shifts = (0, -1, 1, 2)

    def xy_copy(h, stage, kind):
        first = h
        second = 1 - h
        axis = first if stage == 0 else second
        r = 0 if stage == 0 else shifts[stage - 1]
        b = (0, 0, -1, 1)[kind]
        go = (1, -1, 1, -1)[kind]
        ra, rb = (b, 0) if stage == 0 else (r, b)
        if first == 0:
            rx, ry = ra, rb
        else:
            rx, ry = rb, ra
        block = lax.rem(y + ry + YS, YS) * XS + lax.rem(xq + rx + XS, XS)
        at = pl.ds(pl.multiple_of(block * 32 + h * 16, 16), 16)
        cols = (slice(None), slice(None), pl.ds(0, 2048), pl.ds(2048, 2048))[kind]
        return pltpu.make_async_remote_copy(
            src_ref=xa.at[at, cols], dst_ref=xa.at[at, cols],
            send_sem=xy_send, recv_sem=xy_recv.at[h, stage, min(kind, 2)],
            device_id={"dp": shifted(axis, go) * CORES + core}, device_id_type=MESH)

    def xy_full(h, stage):
        xy_copy(h, stage, 0).start()
        xy_copy(h, stage, 1).start()

    def xy_one(h, stage):
        xy_copy(h, stage, 0).wait_recv()
        xy_copy(h, stage, 2).start()
        if stage == 0:
            xy_full(h, 2)
        xy_copy(h, stage, 1).wait_recv()
        xy_copy(h, stage, 3).start()
        if stage == 0:
            xy_full(h, 3)

    def xy_two(h, stage):
        settle(xa.at[pl.ds(0, 16)], xy_recv.at[h, stage, 2])
        if stage == 0:
            xy_full(h, 4)

    def y_copy(k):
        src = pl.ds(pl.multiple_of(chips[k] * 32, 32), 32)
        return pltpu.make_async_remote_copy(
            src_ref=yb.at[src], dst_ref=out_ref.at[:, chip_cols],
            send_sem=y_send, recv_sem=y_recv,
            device_id={"dp": p_to[k]}, device_id_type=MESH)

    def c_copy(k):
        return pltpu.make_async_remote_copy(
            src_ref=wc_ref.at[:, pl.ds(pl.multiple_of(dp * 128, 128), 128)],
            dst_ref=wz.at[core, y, xq, pl.ds(pl.multiple_of(me * 8, 8), 8)],
            send_sem=c_send, recv_sem=c_recv,
            device_id={"tensor": z_all[k]}, device_id_type=MESH)

    def p_copy(h, phase, k):
        rows = pl.ds(h * 32, 32)
        axis = h if phase == 0 else 1 - h
        if phase == 0:
            at = wz.at[core, y, xq, rows]
        elif axis == 1:
            at = wz.at[core, y, :, rows]
        else:
            at = wz.at[core, :, xq, rows]
        return pltpu.make_async_remote_copy(
            src_ref=at, dst_ref=at, send_sem=p_send.at[h, phase], recv_sem=p_recv.at[h, phase],
            device_id={"dp": shifted(axis, k) * CORES + core}, device_id_type=MESH)

    def k_copy(h):
        at = wz.at[core, :, :, pl.ds(h * 32, 32)]
        return pltpu.make_async_remote_copy(
            src_ref=at, dst_ref=at, send_sem=k_send.at[h], recv_sem=k_recv.at[h],
            device_id={"dp": partner}, device_id_type=MESH)

    def t_copy(k):
        return pltpu.make_async_remote_copy(
            src_ref=tsrc.at[z_all[k]], dst_ref=tdst.at[me], send_sem=t_send, recv_sem=t_recv,
            device_id={"tensor": z_all[k]}, device_id_type=MESH)

    def a_copy(k, src, dst, send, recv):
        return pltpu.make_async_remote_copy(
            src_ref=src, dst_ref=dst, send_sem=send.at[0], recv_sem=recv.at[0],
            device_id={"dp": a_to[k]}, device_id_type=MESH)

    def b_copy(k, src, dst, send, recv):
        return pltpu.make_async_remote_copy(
            src_ref=src, dst_ref=dst, send_sem=send.at[1], recv_sem=recv.at[1],
            device_id={"dp": b_to[k]}, device_id_type=MESH)

    lc.wait()
    for k in range(1, n):
        c_copy(k).start()
    wz[core, y, xq, pl.ds(pl.multiple_of(me * 8, 8), 8)] = wc_ref[:, pl.ds(pl.multiple_of(dp * 128, 128), 128)]
    lx.wait()
    lg.wait()
    xa[mine, own_cols] = x_ref[own, :]
    xt_ref[...] = x_ref[...].T
    settle(wz.at[0, 0, 0, pl.ds(0, 56)], c_recv)
    for h in range(2):
        for k in range(1, 4):
            p_copy(h, 0, k).start()
    for k in range(1, n):
        xz_copy(k).start()
    g_step(0)
    le.wait()
    se_ref[...] = jnp.zeros_like(se_ref)

    def sketch_error(low, high):
        @pl.loop(low, high, step=TILE)
        def _(c):
            cols = pl.ds(pl.multiple_of(c, TILE), TILE)
            se_ref[...] += nt(split3(wc_ref[:, cols]), e_ref[:, cols])

    sketch_error(0, 2048)
    for h in range(2):
        settle(wz.at[0, 0, pl.ds(0, 3), pl.ds(0, 32)], p_recv.at[h, 0])
        for k in range(1, 4):
            p_copy(h, 1, k).start()
    sketch_error(2048, 4096)
    for h in range(2):
        settle(wz.at[0, pl.ds(0, 3), :, pl.ds(0, 32)], p_recv.at[h, 1])
        k_copy(h).start()
    for h in range(2):
        k_copy(h).wait_recv()
    for d in range(DP):
        w3_ref[:, d * 128 : d * 128 + 128] = split3(wz[d % CORES, d // PLANE, d % PLANE // CORES])
    lp.wait()
    partial = sum3(nt(w3_ref[...], gpad[...]))
    for t in range(n):
        tsrc[t] = partial[t * 8 : t * 8 + 8]
    for k in range(1, n):
        t_copy(k).start()
    tdst[me] = tsrc[me]
    settle(xa.at[pl.ds(0, 32), pl.ds(0, 3584)], xz_recv)
    for h in range(2):
        xy_full(h, 0)
    for h in range(2):
        xy_full(h, 1)
    g_step(1)
    settle(tdst.at[pl.ds(0, 7)], t_recv)
    tokens = jnp.concatenate(
        [tdst[0] + tdst[1] + tdst[2] + tdst[3], tdst[4] + tdst[5] + tdst[6] + tdst[7]], axis=1)
    sketch = sum3(se_ref[...]) + sum3(nn(split3(tokens), x_ref[...]))
    ks_a, ks_b = range(1, PLANE), range(1, YS)
    sk_src[0] = sketch
    for k in ks_a:
        a_copy(k, sk_src.at[0], abuf.at[xc], sk_send, sk_recv).start()
    abuf[xc] = sketch
    for h in range(2):
        xy_one(h, 0)
    for h in range(2):
        xy_one(h, 1)
    g_step(2)
    settle(abuf.at[pl.ds(0, PLANE - 1)], sk_recv.at[0])
    total = abuf[0]
    for k in range(1, PLANE):
        total += abuf[k]
    sk_src[1] = total
    for k in ks_b:
        b_copy(k, sk_src.at[1], bbuf.at[y], sk_send, sk_recv).start()
    bbuf[y] = total
    for h in range(2):
        xy_two(h, 0)
    for h in range(2):
        xy_two(h, 1)
    g_step(3)
    lw.wait()
    w_step(0)
    settle(bbuf.at[pl.ds(0, YS - 1)], sk_recv.at[1])
    total = bbuf[0]
    for k in range(1, YS):
        total += bbuf[k]
    unit = orthonormal(total)
    u_ref[...] = unit
    u3 = split3(unit)
    v3 = split3(sum3(nt(u3, x_ref[...])))

    @pl.loop(0, 4096, step=TILE)
    def _(c):
        cols = pl.ds(pl.multiple_of(c, TILE), TILE)
        cbuf[:, cols] = sum3(nn(u3, e_ref[:, cols]))

    for h in range(2):
        xy_one(h, 2)
    for h in range(2):
        xy_one(h, 3)
    g_step(4)

    @pl.loop(0, 4096, step=TILE)
    def _(c):
        cols = pl.ds(pl.multiple_of(c, TILE), TILE)
        cbuf[:, cols] += sum3(nn(v3, gbuf[:, cols]))

    def piece(j):
        return pl.ds(pl.multiple_of(j * 128, 128), 128)

    my_piece = piece(dp)

    def r_copy(k):
        return pltpu.make_async_remote_copy(
            src_ref=cbuf.at[:, piece(d_to[k])], dst_ref=cin.at[dp],
            send_sem=cf_send.at[0], recv_sem=cf_recv.at[0],
            device_id={"dp": d_to[k]}, device_id_type=MESH)

    def s_copy(k):
        return pltpu.make_async_remote_copy(
            src_ref=coef_ref.at[:, my_piece], dst_ref=coef_ref.at[:, my_piece],
            send_sem=cf_send.at[1], recv_sem=cf_recv.at[1],
            device_id={"dp": d_to[k]}, device_id_type=MESH)

    for k in range(1, DP):
        r_copy(k).start()
    cin[dp] = cbuf[:, my_piece]
    w_step(1)
    for h in range(2):
        xy_one(h, 4)

    def merge(low, high):
        @pl.loop(low, high, step=TILE)
        def _(c):
            cols = pl.ds(pl.multiple_of(c, TILE), TILE)
            merged_ref[:, cols] = e_ref[:, cols].astype(F32) + nn(xt_ref[...], gbuf[:, cols])

    def product(shift, first=False):
        t = lax.rem(me + shift + n, n)
        at = pl.ds(pl.multiple_of(t * 512, 512), 512)

        @pl.loop(0, 512, step=256)
        def _(r):
            rows = pl.ds(pl.multiple_of(r, 256), 256)
            part = nn(xa[rows, at], wp[at, :])
            yacc[rows, :] = part if first else yacc[rows, :] + part

    def w_ready(s):
        settle(wp.at[pl.ds(0, 1024 if s < 3 else 512), pl.ds(0, 128)], wc_recv.at[s])

    merge(0, 2048)
    w_step(2)
    settle(cin.at[pl.ds(0, DP - 1)], cf_recv.at[0])
    total = cin[0]
    for k in range(1, DP):
        total += cin[k]
    coef_ref[:, my_piece] = total * (1.0 / 32)
    for k in range(1, DP):
        s_copy(k).start()
    merge(2048, 4096)
    for h in range(2):
        for stage in range(2, 5):
            xy_two(h, stage)
    product(0, True)
    w_step(3)
    for s in range(2):
        w_ready(s)
        product(s + 1)
        product(-s - 1)
    w_step(4)
    w_ready(2)
    product(3)
    product(-3)
    w_ready(3)
    product(4)
    yb[...] = yacc[...].astype(BF16)
    for k in range(1, XS * YS):
        y_copy(k).start()
    out_ref[:, chip_cols] = yb[mine, :]
    settle(coef_ref.at[:, pl.ds(0, 128 * (DP - 1))], cf_recv.at[1])
    settle(cbuf.at[:, pl.ds(0, 128 * (DP - 1))], cf_send.at[0])
    settle(coef_ref.at[:, pl.ds(0, 128 * (DP - 1))], cf_send.at[1])
    settle(abuf.at[pl.ds(0, PLANE - 1)], sk_send.at[0])
    settle(bbuf.at[pl.ds(0, YS - 1)], sk_send.at[1])
    settle(xa.at[pl.ds(0, 32), pl.ds(0, 3584)], xz_send)
    settle(wz.at[0, 0, 0, pl.ds(0, 56)], c_send)
    settle(tdst.at[pl.ds(0, 7)], t_send)
    for h in range(2):
        k_copy(h).wait_send()
        settle(wz.at[0, 0, pl.ds(0, 3), pl.ds(0, 32)], p_send.at[h, 0])
        settle(wz.at[0, pl.ds(0, 3), :, pl.ds(0, 32)], p_send.at[h, 1])
    settle(gbuf.at[pl.ds(0, 224)], g_send)
    settle(wp.at[pl.ds(0, 3584), pl.ds(0, 128)], w_send)
    settle(wp.at[pl.ds(0, 3584), pl.ds(0, 128)], wc_send)
    settle(xa.at[pl.ds(0, 480)], xy_send)
    settle(yb.at[pl.ds(0, 480)], y_recv)
    settle(yb.at[pl.ds(0, 480)], y_send)


def error_kernel(m_ref, u_ref, c_ref, y_ref, o_hbm, out_hbm, coef_hbm, basis_hbm, o_ref, basis_ref, sem, o_sem):
    basis_ref[...] = u_ref[...] * math.sqrt(512)
    through = [pltpu.make_async_copy(a, b, sem.at[i]) for i, (a, b) in enumerate(
        ((y_ref, out_hbm), (c_ref, coef_hbm), (basis_ref, basis_hbm)))]
    for c in through:
        c.start()
    u0, u1, u2 = pieces(u_ref[...])
    left = jnp.concatenate([u0, u0, u1, u0, u2, u1], axis=0).T.astype(BF16)
    width = 4096 // PARTS
    stores = []
    for i in range(PARTS):
        cols = pl.ds(i * width, width)
        c0, c1, c2 = pieces(c_ref[:, cols])
        right = jnp.concatenate([c0, c1, c0, c2, c0, c1], axis=0).astype(BF16)
        for r in range(0, 512, 256):
            for c in range(0, width, 256):
                at = (slice(r, r + 256), pl.ds(i * width + c, 256))
                o_ref[at] = (m_ref[at] - nn(left[r : r + 256], right[:, c : c + 256])).astype(BF16)
        stores.append(pltpu.make_async_copy(o_ref.at[:, cols], o_hbm.at[:, cols], o_sem.at[i]))
        stores[i].start()
    for c in stores + through:
        c.wait()


def shards(inputs, weight, out_grad, error_feedback, warm_coeffs):
    S = jax.ShapeDtypeStruct
    V = pl.BlockSpec(memory_space=pltpu.VMEM)
    A = pl.BlockSpec(memory_space=pl.ANY)
    D = pltpu.SemaphoreType.DMA
    VM = pltpu.VMEM
    hbm = lambda v: pltpu.with_memory_space_constraint(v, pltpu.HBM)
    operands = [hbm(v) for v in (inputs, weight, out_grad, error_feedback[0], warm_coeffs[0])]
    out, coef, merged, unit = pl.pallas_call(
        main_kernel,
        out_shape=(VM((32, 4096), BF16), VM((8, 4096), F32), VM((512, 4096), F32), VM((8, 512), F32)),
        in_specs=[A, A, A, A, A],
        out_specs=(V, V, V, V),
        scratch_shapes=[
            VM((256, 512), BF16),
            VM((512, 4096), BF16),
            VM((256, 4096), BF16),
            VM((512, 4096), BF16),
            VM((4096, 256), BF16),
            VM((512, 256), F32),
            VM((512, 256), BF16),
            VM((8, 4096), F32),
            VM((CORES, YS, XS, 64, 128), F32),
            VM((192, 4096), BF16),
            VM((128, 4096), BF16),
            VM((8, 8, 128), F32),
            VM((8, 8, 128), F32),
            VM((24, 512), F32),
            VM((512, 256), BF16),
            VM((8, 4096), F32),
            VM((PLANE, 8, 512), F32),
            VM((YS, 8, 512), F32),
            VM((DP, 8, 128), F32),
            VM((2, 8, 512), F32),
            D((6,)),
            D, D((2, 2, 4)),
            D, D,
            D, D((2, 5, 3)),
            D, D((2, 2, 4)),
            D, D((4,)),
            D, D,
            D((2,)), D((2,)),
            D((2,)), D((2,)),
            D, D,
            D((2, 2)), D((2, 2)),
            D((2,)), D((2,)),
            D, D,
        ],
        compiler_params=pltpu.CompilerParams(
            collective_id=0, has_side_effects=True, vmem_limit_bytes=40 * 2**20),
    )(*operands)
    err, out, coef, basis = pl.pallas_call(
        error_kernel,
        out_shape=(S((512, 4096), BF16), S((32, 4096), BF16), S((8, 4096), F32), S((8, 512), F32)),
        in_specs=[V, V, V, V],
        out_specs=(A, A, A, A),
        scratch_shapes=[VM((512, 4096), BF16), VM((8, 512), F32), D((3,)), D((PARTS,))],
        compiler_params=pltpu.CompilerParams(vmem_limit_bytes=24 * 2**20),
    )(merged, unit, coef, out)
    return (out, basis, coef[None], err[None])


def solution(mesh):
    in_specs = (
        P("dp", "tensor"),
        P("tensor", None),
        P(("dp", "tensor"), None),
        P("dp", "tensor", None),
        P("tensor", None, None),
    )
    out_specs = (
        P(("dp", "tensor"), None),
        P(None, "tensor"),
        P("tensor", None, None),
        P("dp", "tensor", None),
    )
    return jax.shard_map(shards, mesh=mesh, in_specs=in_specs, out_specs=out_specs, check_vma=False)
```

```python
import functools
import math

import jax
import jax.numpy as jnp
from jax import lax
from jax.experimental import pallas as pl
from jax.experimental.pallas import tpu as pltpu
from jax.sharding import PartitionSpec as P

MESH = pl.DeviceIdType.MESH
F32 = jnp.float32
BF16 = jnp.bfloat16
EPSILON = 1e-06
TILE = 512
PARTS = 4
SLOTS = (0, -1, 1, 2, -2, 3, -3, 4)
XS, YS, CORES = 4, 4, 2
PLANE = XS * CORES
DP = YS * PLANE
OFFSETS = sorted(
    ((dy, dx, dc) for dy in range(YS) for dx in range(XS) for dc in range(CORES)),
    key=lambda o: (-min(o[0], YS - o[0]) - min(o[1], XS - o[1]), -o[2]))


def nn(a, b):
    return lax.dot_general(a, b, (((1,), (0,)), ((), ())), preferred_element_type=F32)


def nt(a, b):
    return lax.dot_general(a, b, (((1,), (1,)), ((), ())), preferred_element_type=F32)


def pieces(v):
    high = v.astype(BF16).astype(F32)
    rest = v - high
    middle = rest.astype(BF16).astype(F32)
    return high, middle, rest - middle


def split3(v):
    return jnp.concatenate(pieces(v), axis=0).astype(BF16)


def sum3(v):
    n = v.shape[0] // 3
    return v[:n] + v[n : 2 * n] + v[2 * n :]


def orthonormal(v):
    rows = lax.broadcasted_iota(jnp.int32, (v.shape[0], 1), 0)
    for i in range(v.shape[0]):
        row = v[i : i + 1]
        dots = jnp.sum(v * row, axis=1, keepdims=True)
        scale = lax.rsqrt(dots[i : i + 1] + EPSILON)
        unit = row * scale
        v = jnp.where(rows == i, unit, jnp.where(rows > i, v - (dots * scale) * unit, v))
    return v


def main_kernel(
    x_hbm, w_hbm, g_hbm, e_hbm, wc_hbm,
    out_ref, coef_ref, merged_ref, u_ref,
    x_ref, e_ref, gbuf, xa, wp, yacc, yb, wc_ref, wz, w3_ref, gpad, tsrc, tdst, se_ref, xt_ref, cbuf,
    abuf, bbuf, cin, sk_src,
    lsem, g_send, g_recv, xz_send, xz_recv, xy_send, xy_recv, w_send, w_recv, wc_send, wc_recv,
    y_send, y_recv, sk_send, sk_recv, cf_send, cf_recv, c_send, c_recv, p_send, p_recv, k_send, k_recv,
    t_send, t_recv,
):
    n = 8
    me = lax.axis_index("tensor")
    dp = lax.axis_index("dp")
    core = dp % CORES
    chip = dp // CORES
    y, xc = dp // PLANE, dp % PLANE
    xq = xc // CORES
    z_all = [lax.rem(me + k, n) for k in range(n)]
    z_to = [z_all[1], z_all[n - 1]]
    sign = (1, -1)
    a_to = [y * PLANE + lax.rem(xc + k, PLANE) for k in range(PLANE)]
    b_to = [lax.rem(y + k, YS) * PLANE + xc for k in range(YS)]
    d_to = [lax.rem(y + dy, YS) * PLANE + lax.rem(xq + dx, XS) * CORES + lax.rem(core + dc, CORES) for dy, dx, dc in OFFSETS]
    chips = [lax.rem(y + dy, YS) * XS + lax.rem(xq + dx, XS) for dy, dx, dc in OFFSETS if dc == 0]
    p_to = [c * CORES + core for c in chips]
    partner = chip * CORES + (1 - core)

    def shifted(axis, r):
        if axis == 0:
            return y * XS + lax.rem(xq + r + XS, XS)
        return lax.rem(y + r + YS, YS) * XS + xq

    own = pl.ds(pl.multiple_of(me * 32, 32), 32)
    mine = pl.ds(pl.multiple_of(chip * 32, 32), 32)
    own_cols = pl.ds(pl.multiple_of(me * 512, 512), 512)
    own_rows = own_cols
    chip_cols = pl.ds(pl.multiple_of(chip * 256, 256), 256)
    lx = pltpu.make_async_copy(x_hbm, x_ref, lsem.at[0])
    lw = [pltpu.make_async_copy(
        w_hbm.at[:, pl.ds(pl.multiple_of(chip * 256 + c * 128, 128), 128)], wp.at[c, own_rows], lsem.at[1 + 5 * c])
        for c in range(CORES)]
    le = pltpu.make_async_copy(e_hbm, e_ref, lsem.at[2])
    lg = pltpu.make_async_copy(g_hbm, gbuf.at[own], lsem.at[3])
    lc = pltpu.make_async_copy(wc_hbm, wc_ref, lsem.at[5])
    lp = pltpu.make_async_copy(g_hbm, gpad.at[pl.ds(pl.multiple_of(lax.rem(me, 4) * 32, 32), 32)], lsem.at[4])
    for c in (lc, lx, lg, le, *lw):
        c.start()

    barrier = pltpu.get_barrier_semaphore()
    for z in z_all[1:]:
        pl.semaphore_signal(barrier, inc=1, device_id={"tensor": z}, device_id_type=MESH)
    for d in d_to[:-1]:
        pl.semaphore_signal(barrier, inc=1, device_id={"dp": d}, device_id_type=MESH)
    gpad[...] = jnp.zeros_like(gpad)
    lp.start()
    pl.semaphore_wait(barrier, 7 + 31)

    def settle(ref, sem):
        pltpu.make_async_copy(ref, ref, sem).wait()

    def steps(d, h):
        return 4 if d == h else 3

    def ring_copy(buf, rows, part, send, recv, d, h, s):
        block = lax.rem(me - sign[d] * s + n, n)
        at = pl.ds(pl.multiple_of(block * rows + h * part, part), part)
        return pltpu.make_async_remote_copy(
            src_ref=buf.at[at], dst_ref=buf.at[at],
            send_sem=send, recv_sem=recv.at[d, h, s],
            device_id={"tensor": z_to[d]}, device_id_type=MESH)

    def g_copy(d, h, s):
        return ring_copy(gbuf, 32, 16, g_send, g_recv, d, h, s)

    def w_copy(d, h, s):
        return ring_copy(wp.at[core], 512, 256, w_send, w_recv, d, h, s)

    def wc_copy(d, h, s):
        block = lax.rem(me - sign[d] * (s + 1) + n, n)
        at = pl.ds(pl.multiple_of(block * 512 + h * 256, 256), 256)
        return pltpu.make_async_remote_copy(
            src_ref=wp.at[core, at], dst_ref=wp.at[core, at],
            send_sem=wc_send, recv_sem=wc_recv.at[s],
            device_id={"dp": partner}, device_id_type=MESH)

    def g_step(s):
        for h in range(2):
            for d in range(2):
                if s > 0 and s - 1 < steps(d, h):
                    g_copy(d, h, s - 1).wait_recv()
                if s < steps(d, h):
                    g_copy(d, h, s).start()

    def w_step(s):
        for h in range(2):
            for d in range(2):
                if s > 0 and s - 1 < steps(d, h):
                    w_copy(d, h, s - 1).wait_recv()
                if s < steps(d, h):
                    w_copy(d, h, s).start()
                if s > 0 and s - 1 < steps(d, h):
                    wc_copy(d, h, s - 1).start()

    def slot_cols(shift):
        return pl.ds(SLOTS.index(shift) * 512, 512)

    def xz_copy(k):
        src = pl.ds(pl.multiple_of(lax.rem(me + k + n, n) * 32, 32), 32)
        there = 4 if k == 4 else -k
        return pltpu.make_async_remote_copy(
            src_ref=x_ref.at[src], dst_ref=xa.at[mine, slot_cols(there)],
            send_sem=xz_send, recv_sem=xz_recv.at[SLOTS.index(there) // 4],
            device_id={"tensor": lax.rem(me + k + n, n)}, device_id_type=MESH)

    shifts = (0, -1, 1, 2)

    def xy_copy(h, stage, kind):
        first = h
        second = 1 - h
        axis = first if stage == 0 else second
        r = 0 if stage == 0 else shifts[stage - 1]
        b = (0, 0, -1, 1)[kind]
        go = (1, -1, 1, -1)[kind]
        ra, rb = (b, 0) if stage == 0 else (r, b)
        if first == 0:
            rx, ry = ra, rb
        else:
            rx, ry = rb, ra
        block = lax.rem(y + ry + YS, YS) * XS + lax.rem(xq + rx + XS, XS)
        at = pl.ds(pl.multiple_of(block * 32 + (16 if kind == 3 else 0), 16), 32 if kind < 2 else 16)
        cols = pl.ds(h * 2048, 2048)
        return pltpu.make_async_remote_copy(
            src_ref=xa.at[at, cols], dst_ref=xa.at[at, cols],
            send_sem=xy_send, recv_sem=xy_recv.at[h, stage, min(kind, 2)],
            device_id={"dp": shifted(axis, go) * CORES + core}, device_id_type=MESH)

    def xy_full(h, stage):
        xy_copy(h, stage, 0).start()
        xy_copy(h, stage, 1).start()

    def xy_one(h, stage):
        xy_copy(h, stage, 0).wait_recv()
        xy_copy(h, stage, 2).start()
        xy_copy(h, stage, 1).wait_recv()
        xy_copy(h, stage, 3).start()

    def xy_two(h, stage):
        settle(xa.at[pl.ds(0, 32), pl.ds(0, 2048)], xy_recv.at[h, stage, 2])
        if stage == 0:
            xy_full(h, 4)

    def y_copy(k):
        src = pl.ds(pl.multiple_of(chips[k] * 32, 32), 32)
        return pltpu.make_async_remote_copy(
            src_ref=yb.at[src], dst_ref=out_ref.at[:, chip_cols],
            send_sem=y_send, recv_sem=y_recv,
            device_id={"dp": p_to[k]}, device_id_type=MESH)

    def c_copy(k):
        return pltpu.make_async_remote_copy(
            src_ref=wc_ref.at[:, pl.ds(pl.multiple_of(dp * 128, 128), 128)],
            dst_ref=wz.at[core, y, xq, pl.ds(pl.multiple_of(me * 8, 8), 8)],
            send_sem=c_send, recv_sem=c_recv,
            device_id={"tensor": z_all[k]}, device_id_type=MESH)

    def p_copy(h, phase, k):
        rows = pl.ds(h * 32, 32)
        axis = h if phase == 0 else 1 - h
        if phase == 0:
            at = wz.at[core, y, xq, rows]
        elif axis == 1:
            at = wz.at[core, y, :, rows]
        else:
            at = wz.at[core, :, xq, rows]
        return pltpu.make_async_remote_copy(
            src_ref=at, dst_ref=at, send_sem=p_send.at[h, phase], recv_sem=p_recv.at[h, phase],
            device_id={"dp": shifted(axis, k) * CORES + core}, device_id_type=MESH)

    def k_copy(h):
        at = wz.at[core, :, :, pl.ds(h * 32, 32)]
        return pltpu.make_async_remote_copy(
            src_ref=at, dst_ref=at, send_sem=k_send.at[h], recv_sem=k_recv.at[h],
            device_id={"dp": partner}, device_id_type=MESH)

    def t_copy(k):
        return pltpu.make_async_remote_copy(
            src_ref=tsrc.at[z_all[k]], dst_ref=tdst.at[me], send_sem=t_send, recv_sem=t_recv,
            device_id={"tensor": z_all[k]}, device_id_type=MESH)

    def a_copy(k, src, dst, send, recv):
        return pltpu.make_async_remote_copy(
            src_ref=src, dst_ref=dst, send_sem=send.at[0], recv_sem=recv.at[0],
            device_id={"dp": a_to[k]}, device_id_type=MESH)

    def b_copy(k, src, dst, send, recv):
        return pltpu.make_async_remote_copy(
            src_ref=src, dst_ref=dst, send_sem=send.at[1], recv_sem=recv.at[1],
            device_id={"dp": b_to[k]}, device_id_type=MESH)

    def merge(low, high):
        @pl.loop(low, high, step=TILE)
        def _(c):
            cols = pl.ds(pl.multiple_of(c, TILE), TILE)
            merged_ref[:, cols] = e_ref[:, cols].astype(F32) + nn(xt_ref[...], gbuf[:, cols])

    def product(shift, first=False):
        t = lax.rem(me + shift + n, n)
        at = pl.ds(pl.multiple_of(t * 512, 512), 512)

        @pl.loop(0, 512, step=256)
        def _(r):
            rows = pl.ds(pl.multiple_of(r, 256), 256)
            strips = jnp.concatenate([wp[0, at], wp[1, at]], axis=1)
            part = nn(xa[rows, slot_cols(shift)], strips)
            yacc[rows, :] = part if first else yacc[rows, :] + part

    def w_ready(s):
        settle(wp.at[0, pl.ds(0, 1024 if s < 3 else 512)], wc_recv.at[s])

    def piece(j):
        return pl.ds(pl.multiple_of(j * 128, 128), 128)

    my_piece = piece(dp)

    def r_copy(to):
        return pltpu.make_async_remote_copy(
            src_ref=cbuf.at[:, piece(to)], dst_ref=cin.at[dp],
            send_sem=cf_send.at[0], recv_sem=cf_recv.at[0],
            device_id={"dp": to}, device_id_type=MESH)

    def s_copy(k):
        return pltpu.make_async_remote_copy(
            src_ref=coef_ref.at[:, my_piece], dst_ref=coef_ref.at[:, my_piece],
            send_sem=cf_send.at[1], recv_sem=cf_recv.at[1],
            device_id={"dp": d_to[k]}, device_id_type=MESH)

    lc.wait()
    for k in range(1, n):
        c_copy(k).start()
    wz[core, y, xq, pl.ds(pl.multiple_of(me * 8, 8), 8)] = wc_ref[:, pl.ds(pl.multiple_of(dp * 128, 128), 128)]
    lx.wait()
    for k in (1, -1, -2, 2, -3, 3, 4):
        xz_copy(k).start()
    lg.wait()
    g_step(0)
    for c in lw:
        c.wait()
    w_step(0)
    xa[mine, slot_cols(0)] = x_ref[own, :]
    xt_ref[...] = x_ref[...].T
    settle(wz.at[0, 0, 0, pl.ds(0, 56)], c_recv)
    for h in range(2):
        for k in range(1, 4):
            p_copy(h, 0, k).start()
    settle(xa.at[pl.ds(0, 32), pl.ds(0, 1536)], xz_recv.at[0])
    xy_full(0, 0)
    xy_full(0, 1)
    le.wait()
    se_ref[...] = jnp.zeros_like(se_ref)

    def sketch_error(low, high):
        @pl.loop(low, high, step=TILE)
        def _(c):
            cols = pl.ds(pl.multiple_of(c, TILE), TILE)
            se_ref[...] += nt(split3(wc_ref[:, cols]), e_ref[:, cols])

    sketch_error(0, 2048)
    for h in range(2):
        settle(wz.at[0, 0, pl.ds(0, 3), pl.ds(0, 32)], p_recv.at[h, 0])
        for k in range(1, 4):
            p_copy(h, 1, k).start()
    settle(xa.at[pl.ds(0, 32), pl.ds(0, 2048)], xz_recv.at[1])
    xy_full(1, 0)
    xy_full(1, 1)
    xy_one(0, 0)
    xy_full(0, 2)
    xy_one(0, 1)
    sketch_error(2048, 4096)
    g_step(1)
    for h in range(2):
        settle(wz.at[0, pl.ds(0, 3), :, pl.ds(0, 32)], p_recv.at[h, 1])
        k_copy(h).start()
    for h in range(2):
        k_copy(h).wait_recv()
    for d in range(DP):
        w3_ref[:, d * 128 : d * 128 + 128] = split3(wz[d % CORES, d // PLANE, d % PLANE // CORES])
    lp.wait()
    partial = sum3(nt(w3_ref[...], gpad[...]))
    for t in range(n):
        tsrc[t] = partial[t * 8 : t * 8 + 8]
    for k in range(1, n):
        t_copy(k).start()
    tdst[me] = tsrc[me]
    xy_one(1, 0)
    xy_full(1, 2)
    xy_full(0, 3)
    xy_full(1, 3)
    w_step(1)
    xy_two(0, 0)
    xy_one(1, 1)
    settle(tdst.at[pl.ds(0, 7)], t_recv)
    tokens = jnp.concatenate(
        [tdst[0] + tdst[1] + tdst[2] + tdst[3], tdst[4] + tdst[5] + tdst[6] + tdst[7]], axis=1)
    sketch = sum3(se_ref[...]) + sum3(nn(split3(tokens), x_ref[...]))
    ks_a, ks_b = range(1, PLANE), range(1, YS)
    sk_src[0] = sketch
    for k in ks_a:
        a_copy(k, sk_src.at[0], abuf.at[xc], sk_send, sk_recv).start()
    abuf[xc] = sketch
    g_step(2)
    xy_two(1, 0)
    xy_one(0, 2)
    xy_one(1, 2)
    settle(abuf.at[pl.ds(0, PLANE - 1)], sk_recv.at[0])
    total = abuf[0]
    for k in range(1, PLANE):
        total += abuf[k]
    sk_src[1] = total
    for k in ks_b:
        b_copy(k, sk_src.at[1], bbuf.at[y], sk_send, sk_recv).start()
    bbuf[y] = total
    w_step(2)
    xy_one(0, 3)
    xy_one(1, 3)
    g_step(3)
    xy_one(0, 4)
    xy_one(1, 4)
    settle(bbuf.at[pl.ds(0, YS - 1)], sk_recv.at[1])
    total = bbuf[0]
    for k in range(1, YS):
        total += bbuf[k]
    unit = orthonormal(total)
    u_ref[...] = unit
    u3 = split3(unit)
    v3 = split3(sum3(nt(u3, x_ref[...])))

    @pl.loop(0, 4096, step=TILE)
    def _(c):
        cols = pl.ds(pl.multiple_of(c, TILE), TILE)
        cbuf[:, cols] = sum3(nn(u3, e_ref[:, cols]))

    w_step(3)
    for h in range(2):
        for stage in range(1, 5):
            xy_two(h, stage)
    product(0, True)
    w_ready(0)
    product(1)
    product(-1)
    w_ready(1)
    product(2)
    product(-2)
    g_step(4)

    def coefficients(row):
        @pl.loop(0, 1024, step=TILE)
        def _(c):
            cols = pl.ds(pl.multiple_of(row * 1024 + c, TILE), TILE)
            cbuf[:, cols] += sum3(nn(v3, gbuf[:, cols]))

    for dy in (2, 1, 3):
        row = lax.rem(y + dy, YS)
        coefficients(row)
        for j in range(PLANE):
            r_copy(row * PLANE + j).start()
    coefficients(y)
    for k in ks_a:
        r_copy(a_to[k]).start()
    cin[dp] = cbuf[:, my_piece]
    w_step(4)
    w_ready(2)
    product(3)
    product(-3)
    w_ready(3)
    product(4)
    yb[...] = yacc[...].astype(BF16)
    for k in range(XS * YS - 1):
        y_copy(k).start()
    out_ref[:, chip_cols] = yb[mine, :]
    settle(cin.at[pl.ds(0, DP - 1)], cf_recv.at[0])
    total = cin[0]
    for k in range(1, DP):
        total += cin[k]
    coef_ref[:, my_piece] = total * (1.0 / 32)
    for k in range(DP - 1):
        s_copy(k).start()
    merge(0, 4096)
    settle(coef_ref.at[:, pl.ds(0, 128 * (DP - 1))], cf_recv.at[1])
    settle(cbuf.at[:, pl.ds(0, 128 * (DP - 1))], cf_send.at[0])
    settle(coef_ref.at[:, pl.ds(0, 128 * (DP - 1))], cf_send.at[1])
    settle(abuf.at[pl.ds(0, PLANE - 1)], sk_send.at[0])
    settle(bbuf.at[pl.ds(0, YS - 1)], sk_send.at[1])
    settle(xa.at[pl.ds(0, 32), pl.ds(0, 3584)], xz_send)
    settle(wz.at[0, 0, 0, pl.ds(0, 56)], c_send)
    settle(tdst.at[pl.ds(0, 7)], t_send)
    for h in range(2):
        k_copy(h).wait_send()
        settle(wz.at[0, 0, pl.ds(0, 3), pl.ds(0, 32)], p_send.at[h, 0])
        settle(wz.at[0, pl.ds(0, 3), :, pl.ds(0, 32)], p_send.at[h, 1])
    settle(gbuf.at[pl.ds(0, 224)], g_send)
    settle(wp.at[0, pl.ds(0, 3584)], w_send)
    settle(wp.at[0, pl.ds(0, 3584)], wc_send)
    settle(xa.at[pl.ds(0, 480)], xy_send)
    settle(yb.at[pl.ds(0, 480)], y_recv)
    settle(yb.at[pl.ds(0, 480)], y_send)


def error_kernel(m_ref, u_ref, c_ref, y_ref, o_hbm, out_hbm, coef_hbm, basis_hbm, o_ref, basis_ref, sem, o_sem):
    basis_ref[...] = u_ref[...] * math.sqrt(512)
    through = [pltpu.make_async_copy(a, b, sem.at[i]) for i, (a, b) in enumerate(
        ((y_ref, out_hbm), (c_ref, coef_hbm), (basis_ref, basis_hbm)))]
    for c in through:
        c.start()
    u0, u1, u2 = pieces(u_ref[...])
    left = jnp.concatenate([u0, u0, u1, u0, u2, u1], axis=0).T.astype(BF16)
    width = 4096 // PARTS
    stores = []
    for i in range(PARTS):
        cols = pl.ds(i * width, width)
        c0, c1, c2 = pieces(c_ref[:, cols])
        right = jnp.concatenate([c0, c1, c0, c2, c0, c1], axis=0).astype(BF16)
        for r in range(0, 512, 256):
            for c in range(0, width, 256):
                at = (slice(r, r + 256), pl.ds(i * width + c, 256))
                o_ref[at] = (m_ref[at] - nn(left[r : r + 256], right[:, c : c + 256])).astype(BF16)
        stores.append(pltpu.make_async_copy(o_ref.at[:, cols], o_hbm.at[:, cols], o_sem.at[i]))
        stores[i].start()
    for c in stores + through:
        c.wait()


def shards(inputs, weight, out_grad, error_feedback, warm_coeffs):
    S = jax.ShapeDtypeStruct
    V = pl.BlockSpec(memory_space=pltpu.VMEM)
    A = pl.BlockSpec(memory_space=pl.ANY)
    D = pltpu.SemaphoreType.DMA
    VM = pltpu.VMEM
    hbm = lambda v: pltpu.with_memory_space_constraint(v, pltpu.HBM)
    operands = [hbm(v) for v in (inputs, weight, out_grad, error_feedback[0], warm_coeffs[0])]
    out, coef, merged, unit = pl.pallas_call(
        main_kernel,
        out_shape=(VM((32, 4096), BF16), VM((8, 4096), F32), VM((512, 4096), F32), VM((8, 512), F32)),
        in_specs=[A, A, A, A, A],
        out_specs=(V, V, V, V),
        scratch_shapes=[
            VM((256, 512), BF16),
            VM((512, 4096), BF16),
            VM((256, 4096), BF16),
            VM((512, 4096), BF16),
            VM((CORES, 4096, 128), BF16),
            VM((512, 256), F32),
            VM((512, 256), BF16),
            VM((8, 4096), F32),
            VM((CORES, YS, XS, 64, 128), F32),
            VM((192, 4096), BF16),
            VM((128, 4096), BF16),
            VM((8, 8, 128), F32),
            VM((8, 8, 128), F32),
            VM((24, 512), F32),
            VM((512, 256), BF16),
            VM((8, 4096), F32),
            VM((PLANE, 8, 512), F32),
            VM((YS, 8, 512), F32),
            VM((DP, 8, 128), F32),
            VM((2, 8, 512), F32),
            D((7,)),
            D, D((2, 2, 4)),
            D, D((2,)),
            D, D((2, 5, 3)),
            D, D((2, 2, 4)),
            D, D((4,)),
            D, D,
            D((2,)), D((2,)),
            D((2,)), D((2,)),
            D, D,
            D((2, 2)), D((2, 2)),
            D((2,)), D((2,)),
            D, D,
        ],
        compiler_params=pltpu.CompilerParams(
            collective_id=0, has_side_effects=True, vmem_limit_bytes=40 * 2**20),
    )(*operands)
    err, out, coef, basis = pl.pallas_call(
        error_kernel,
        out_shape=(S((512, 4096), BF16), S((32, 4096), BF16), S((8, 4096), F32), S((8, 512), F32)),
        in_specs=[V, V, V, V],
        out_specs=(A, A, A, A),
        scratch_shapes=[VM((512, 4096), BF16), VM((8, 512), F32), D((3,)), D((PARTS,))],
        compiler_params=pltpu.CompilerParams(vmem_limit_bytes=24 * 2**20),
    )(merged, unit, coef, out)
    return (out, basis, coef[None], err[None])


def solution(mesh):
    in_specs = (
        P("dp", "tensor"),
        P("tensor", None),
        P(("dp", "tensor"), None),
        P("dp", "tensor", None),
        P("tensor", None, None),
    )
    out_specs = (
        P(("dp", "tensor"), None),
        P(None, "tensor"),
        P("tensor", None, None),
        P("dp", "tensor", None),
    )
    return jax.shard_map(shards, mesh=mesh, in_specs=in_specs, out_specs=out_specs, check_vma=False)
```

```python
import functools
import math

import jax
import jax.numpy as jnp
from jax import lax
from jax.experimental import pallas as pl
from jax.experimental.pallas import tpu as pltpu
from jax.sharding import PartitionSpec as P

MESH = pl.DeviceIdType.MESH
F32 = jnp.float32
BF16 = jnp.bfloat16
EPSILON = 1e-06
TILE = 512
PARTS = 8
SLOTS = (0, -1, 1, 2, -2, 3, -3, 4)
XS, YS, CORES = 4, 4, 2
PLANE = XS * CORES
DP = YS * PLANE
OFFSETS = sorted(
    ((dy, dx, dc) for dy in range(YS) for dx in range(XS) for dc in range(CORES)),
    key=lambda o: (-min(o[0], YS - o[0]) - min(o[1], XS - o[1]), -o[2]))


def nn(a, b):
    return lax.dot_general(a, b, (((1,), (0,)), ((), ())), preferred_element_type=F32)


def nt(a, b):
    return lax.dot_general(a, b, (((1,), (1,)), ((), ())), preferred_element_type=F32)


def pieces(v):
    high = v.astype(BF16).astype(F32)
    rest = v - high
    middle = rest.astype(BF16).astype(F32)
    return high, middle, rest - middle


def split3(v):
    return jnp.concatenate(pieces(v), axis=0).astype(BF16)


def sum3(v):
    n = v.shape[0] // 3
    return v[:n] + v[n : 2 * n] + v[2 * n :]


def orthonormal(v):
    rows = lax.broadcasted_iota(jnp.int32, (v.shape[0], 1), 0)
    for i in range(v.shape[0]):
        row = v[i : i + 1]
        dots = jnp.sum(v * row, axis=1, keepdims=True)
        scale = lax.rsqrt(dots[i : i + 1] + EPSILON)
        unit = row * scale
        v = jnp.where(rows == i, unit, jnp.where(rows > i, v - (dots * scale) * unit, v))
    return v


def main_kernel(
    x_hbm, w_hbm, g_hbm, e_hbm, wc_hbm,
    out_ref, coef_ref, merged_ref, u_ref,
    x_ref, e_ref, gbuf, xa, wp, yacc, yb, wc_ref, wz, w3_ref, gpad, tsrc, tdst, se_ref, xt_ref, cbuf,
    abuf, bbuf, cin, sk_src,
    lsem, g_send, g_recv, xz_send, xz_recv, xy_send, xy_recv, w_send, w_recv, wc_send, wc_recv,
    y_send, y_recv, sk_send, sk_recv, cf_send, cf_recv, c_send, c_recv, p_send, p_recv, k_send, k_recv,
    t_send, t_recv,
):
    n = 8
    me = lax.axis_index("tensor")
    dp = lax.axis_index("dp")
    core = dp % CORES
    chip = dp // CORES
    y, xc = dp // PLANE, dp % PLANE
    xq = xc // CORES
    z_all = [lax.rem(me + k, n) for k in range(n)]
    z_to = [z_all[1], z_all[n - 1]]
    sign = (1, -1)
    a_to = [y * PLANE + lax.rem(xc + k, PLANE) for k in range(PLANE)]
    b_to = [lax.rem(y + k, YS) * PLANE + xc for k in range(YS)]
    d_to = [lax.rem(y + dy, YS) * PLANE + lax.rem(xq + dx, XS) * CORES + lax.rem(core + dc, CORES) for dy, dx, dc in OFFSETS]
    chips = [lax.rem(y + dy, YS) * XS + lax.rem(xq + dx, XS) for dy, dx, dc in OFFSETS if dc == 0]
    p_to = [c * CORES + core for c in chips]
    partner = chip * CORES + (1 - core)

    def shifted(axis, r):
        if axis == 0:
            return y * XS + lax.rem(xq + r + XS, XS)
        return lax.rem(y + r + YS, YS) * XS + xq

    own = pl.ds(pl.multiple_of(me * 32, 32), 32)
    mine = pl.ds(pl.multiple_of(chip * 32, 32), 32)
    own_cols = pl.ds(pl.multiple_of(me * 512, 512), 512)
    own_rows = own_cols
    chip_cols = pl.ds(pl.multiple_of(chip * 256, 256), 256)
    lx = pltpu.make_async_copy(x_hbm, x_ref, lsem.at[0])
    lw = [pltpu.make_async_copy(
        w_hbm.at[:, pl.ds(pl.multiple_of(chip * 256 + c * 128, 128), 128)], wp.at[c, own_rows], lsem.at[1 + 5 * c])
        for c in range(CORES)]
    le = pltpu.make_async_copy(e_hbm, e_ref, lsem.at[2])
    lg = pltpu.make_async_copy(g_hbm, gbuf.at[own], lsem.at[3])
    lc = pltpu.make_async_copy(wc_hbm, wc_ref, lsem.at[5])
    lp = pltpu.make_async_copy(g_hbm, gpad.at[pl.ds(pl.multiple_of(lax.rem(me, 4) * 32, 32), 32)], lsem.at[4])
    for c in (lc, lx, lg, le, *lw):
        c.start()

    barrier = pltpu.get_barrier_semaphore()
    for z in z_all[1:]:
        pl.semaphore_signal(barrier, inc=1, device_id={"tensor": z}, device_id_type=MESH)
    for d in d_to[:-1]:
        pl.semaphore_signal(barrier, inc=1, device_id={"dp": d}, device_id_type=MESH)
    gpad[...] = jnp.zeros_like(gpad)
    lp.start()
    pl.semaphore_wait(barrier, 7 + 31)

    def settle(ref, sem):
        pltpu.make_async_copy(ref, ref, sem).wait()

    def steps(d, h):
        return 4 if d == h else 3

    def ring_copy(buf, rows, part, send, recv, d, h, s):
        block = lax.rem(me - sign[d] * s + n, n)
        at = pl.ds(pl.multiple_of(block * rows + h * part, part), part)
        return pltpu.make_async_remote_copy(
            src_ref=buf.at[at], dst_ref=buf.at[at],
            send_sem=send, recv_sem=recv.at[d, h, s],
            device_id={"tensor": z_to[d]}, device_id_type=MESH)

    def g_copy(d, h, s):
        return ring_copy(gbuf, 32, 16, g_send, g_recv, d, h, s)

    def w_copy(d, h, s):
        return ring_copy(wp.at[core], 512, 256, w_send, w_recv, d, h, s)

    def wc_copy(d, h, s):
        block = lax.rem(me - sign[d] * (s + 1) + n, n)
        at = pl.ds(pl.multiple_of(block * 512 + h * 256, 256), 256)
        return pltpu.make_async_remote_copy(
            src_ref=wp.at[core, at], dst_ref=wp.at[core, at],
            send_sem=wc_send, recv_sem=wc_recv.at[s],
            device_id={"dp": partner}, device_id_type=MESH)

    def g_step(s):
        for h in range(2):
            for d in range(2):
                if s > 0 and s - 1 < steps(d, h):
                    g_copy(d, h, s - 1).wait_recv()
                if s < steps(d, h):
                    g_copy(d, h, s).start()

    def w_step(s):
        for h in range(2):
            for d in range(2):
                if s > 0 and s - 1 < steps(d, h):
                    w_copy(d, h, s - 1).wait_recv()
                if s < steps(d, h):
                    w_copy(d, h, s).start()
                if s > 0 and s - 1 < steps(d, h):
                    wc_copy(d, h, s - 1).start()

    def slot_cols(shift):
        return pl.ds(SLOTS.index(shift) * 512, 512)

    def xz_copy(k):
        src = pl.ds(pl.multiple_of(lax.rem(me + k + n, n) * 32, 32), 32)
        there = 4 if k == 4 else -k
        return pltpu.make_async_remote_copy(
            src_ref=x_ref.at[src], dst_ref=xa.at[mine, slot_cols(there)],
            send_sem=xz_send, recv_sem=xz_recv.at[SLOTS.index(there) // 4],
            device_id={"tensor": lax.rem(me + k + n, n)}, device_id_type=MESH)

    shifts = (0, -1, 1, 2)

    def xy_copy(h, stage, kind):
        first = h
        second = 1 - h
        axis = first if stage == 0 else second
        r = 0 if stage == 0 else shifts[stage - 1]
        b = (0, 0, -1, 1)[kind]
        go = (1, -1, 1, -1)[kind]
        ra, rb = (b, 0) if stage == 0 else (r, b)
        if first == 0:
            rx, ry = ra, rb
        else:
            rx, ry = rb, ra
        block = lax.rem(y + ry + YS, YS) * XS + lax.rem(xq + rx + XS, XS)
        at = pl.ds(pl.multiple_of(block * 32 + (16 if kind == 3 else 0), 16), 32 if kind < 2 else 16)
        cols = pl.ds(h * 2048, 2048)
        return pltpu.make_async_remote_copy(
            src_ref=xa.at[at, cols], dst_ref=xa.at[at, cols],
            send_sem=xy_send, recv_sem=xy_recv.at[h, stage, kind // 2],
            device_id={"dp": shifted(axis, go) * CORES + core}, device_id_type=MESH)

    def xy_full(h, stage):
        xy_copy(h, stage, 0).start()
        xy_copy(h, stage, 1).start()

    def xy_one(h, stage):
        settle(xa.at[pl.ds(0, 64), pl.ds(0, 2048)], xy_recv.at[h, stage, 0])
        xy_copy(h, stage, 2).start()
        xy_copy(h, stage, 3).start()

    def xy_two(h, stage):
        settle(xa.at[pl.ds(0, 32), pl.ds(0, 2048)], xy_recv.at[h, stage, 1])
        if stage == 0:
            xy_full(h, 4)

    def y_copy(k):
        src = pl.ds(pl.multiple_of(chips[k] * 32, 32), 32)
        return pltpu.make_async_remote_copy(
            src_ref=yb.at[src], dst_ref=out_ref.at[:, chip_cols],
            send_sem=y_send, recv_sem=y_recv,
            device_id={"dp": p_to[k]}, device_id_type=MESH)

    def c_copy(k):
        return pltpu.make_async_remote_copy(
            src_ref=wc_ref.at[:, pl.ds(pl.multiple_of(dp * 128, 128), 128)],
            dst_ref=wz.at[core, y, xq, pl.ds(pl.multiple_of(me * 8, 8), 8)],
            send_sem=c_send, recv_sem=c_recv,
            device_id={"tensor": z_all[k]}, device_id_type=MESH)

    def p_copy(h, phase, k):
        rows = pl.ds(h * 32, 32)
        axis = h if phase == 0 else 1 - h
        if phase == 0:
            at = wz.at[core, y, xq, rows]
        elif axis == 1:
            at = wz.at[core, y, :, rows]
        else:
            at = wz.at[core, :, xq, rows]
        return pltpu.make_async_remote_copy(
            src_ref=at, dst_ref=at, send_sem=p_send.at[h, phase], recv_sem=p_recv.at[h, phase],
            device_id={"dp": shifted(axis, k) * CORES + core}, device_id_type=MESH)

    def k_copy(h):
        at = wz.at[core, :, :, pl.ds(h * 32, 32)]
        return pltpu.make_async_remote_copy(
            src_ref=at, dst_ref=at, send_sem=k_send, recv_sem=k_recv,
            device_id={"dp": partner}, device_id_type=MESH)

    def t_copy(k):
        return pltpu.make_async_remote_copy(
            src_ref=tsrc.at[z_all[k]], dst_ref=tdst.at[me], send_sem=t_send, recv_sem=t_recv,
            device_id={"tensor": z_all[k]}, device_id_type=MESH)

    def a_copy(k, src, dst, send, recv):
        return pltpu.make_async_remote_copy(
            src_ref=src, dst_ref=dst, send_sem=send.at[0], recv_sem=recv.at[0],
            device_id={"dp": a_to[k]}, device_id_type=MESH)

    def b_copy(k, src, dst, send, recv):
        return pltpu.make_async_remote_copy(
            src_ref=src, dst_ref=dst, send_sem=send.at[1], recv_sem=recv.at[1],
            device_id={"dp": b_to[k]}, device_id_type=MESH)

    def merge(low, high):
        @pl.loop(low, high, step=TILE)
        def _(c):
            cols = pl.ds(pl.multiple_of(c, TILE), TILE)
            merged_ref[:, cols] = e_ref[:, cols].astype(F32) + nn(xt_ref[...], gbuf[:, cols])

    def term(shift):
        t = lax.rem(me + shift + n, n)
        at = pl.ds(pl.multiple_of(t * 512, 512), 512)
        return nn(xa[:, slot_cols(shift)], jnp.concatenate([wp[0, at], wp[1, at]], axis=1))

    def product(*shifts):
        yacc[...] += sum(term(shift) for shift in shifts)

    def w_ready(s):
        settle(wp.at[0, pl.ds(0, 1024 if s < 3 else 512)], wc_recv.at[s])

    def piece(j):
        return pl.ds(pl.multiple_of(j * 128, 128), 128)

    my_piece = piece(dp)

    def r_copy(to):
        return pltpu.make_async_remote_copy(
            src_ref=cbuf.at[:, piece(to)], dst_ref=cin.at[dp],
            send_sem=cf_send.at[0], recv_sem=cf_recv.at[0],
            device_id={"dp": to}, device_id_type=MESH)

    def s_copy(k):
        return pltpu.make_async_remote_copy(
            src_ref=coef_ref.at[:, my_piece], dst_ref=coef_ref.at[:, my_piece],
            send_sem=cf_send.at[1], recv_sem=cf_recv.at[1],
            device_id={"dp": d_to[k]}, device_id_type=MESH)

    lc.wait()
    for k in range(1, n):
        c_copy(k).start()
    wz[core, y, xq, pl.ds(pl.multiple_of(me * 8, 8), 8)] = wc_ref[:, pl.ds(pl.multiple_of(dp * 128, 128), 128)]
    lx.wait()
    for k in (1, -1, -2, 2, -3, 3, 4):
        xz_copy(k).start()
    lg.wait()
    g_step(0)
    for c in lw:
        c.wait()
    w_step(0)
    xa[mine, slot_cols(0)] = x_ref[own, :]
    xt_ref[...] = x_ref[...].T
    settle(wz.at[0, 0, 0, pl.ds(0, 56)], c_recv)
    for h in range(2):
        for k in range(1, 4):
            p_copy(h, 0, k).start()
    settle(xa.at[pl.ds(0, 32), pl.ds(0, 1536)], xz_recv.at[0])
    xy_full(0, 0)
    xy_full(0, 1)
    le.wait()
    se_ref[...] = jnp.zeros_like(se_ref)

    def sketch_error(low, high):
        @pl.loop(low, high, step=TILE)
        def _(c):
            cols = pl.ds(pl.multiple_of(c, TILE), TILE)
            se_ref[...] += nt(split3(wc_ref[:, cols]), e_ref[:, cols])

    sketch_error(0, 2048)
    for h in range(2):
        settle(wz.at[0, 0, pl.ds(0, 3), pl.ds(0, 32)], p_recv.at[h, 0])
        for k in range(1, 4):
            p_copy(h, 1, k).start()
    settle(xa.at[pl.ds(0, 32), pl.ds(0, 2048)], xz_recv.at[1])
    xy_full(1, 0)
    xy_full(1, 1)
    xy_one(0, 0)
    xy_full(0, 2)
    xy_one(0, 1)
    sketch_error(2048, 4096)
    g_step(1)
    for h in range(2):
        settle(wz.at[0, pl.ds(0, 3), :, pl.ds(0, 32)], p_recv.at[h, 1])
        k_copy(h).start()
    settle(wz.at[0], k_recv)
    for d in range(DP):
        w3_ref[:, d * 128 : d * 128 + 128] = split3(wz[d % CORES, d // PLANE, d % PLANE // CORES])
    lp.wait()
    partial = sum3(nt(w3_ref[...], gpad[...]))
    for t in range(n):
        tsrc[t] = partial[t * 8 : t * 8 + 8]
    for k in range(1, n):
        t_copy(k).start()
    tdst[me] = tsrc[me]
    xy_one(1, 0)
    xy_full(1, 2)
    xy_full(0, 3)
    xy_full(1, 3)
    w_step(1)
    xy_two(0, 0)
    xy_one(1, 1)
    g_step(2)
    settle(tdst.at[pl.ds(0, 7)], t_recv)
    tokens = jnp.concatenate(
        [tdst[0] + tdst[1] + tdst[2] + tdst[3], tdst[4] + tdst[5] + tdst[6] + tdst[7]], axis=1)
    sketch = sum3(se_ref[...]) + sum3(nn(split3(tokens), x_ref[...]))
    ks_a, ks_b = range(1, PLANE), range(1, YS)
    sk_src[0] = sketch
    for k in ks_a:
        a_copy(k, sk_src.at[0], abuf.at[xc], sk_send, sk_recv).start()
    abuf[xc] = sketch
    xy_two(1, 0)
    xy_one(0, 2)
    xy_one(1, 2)
    settle(abuf.at[pl.ds(0, PLANE - 1)], sk_recv.at[0])
    total = abuf[0]
    for k in range(1, PLANE):
        total += abuf[k]
    sk_src[1] = total
    for k in ks_b:
        b_copy(k, sk_src.at[1], bbuf.at[y], sk_send, sk_recv).start()
    bbuf[y] = total
    w_step(2)
    xy_one(0, 3)
    xy_one(1, 3)
    g_step(3)
    xy_one(0, 4)
    xy_one(1, 4)
    settle(bbuf.at[pl.ds(0, YS - 1)], sk_recv.at[1])
    total = bbuf[0]
    for k in range(1, YS):
        total += bbuf[k]
    unit = orthonormal(total)
    u_ref[...] = unit
    u3 = split3(unit)
    v3 = split3(sum3(nt(u3, x_ref[...])))

    @pl.loop(0, 4096, step=TILE)
    def _(c):
        cols = pl.ds(pl.multiple_of(c, TILE), TILE)
        cbuf[:, cols] = sum3(nn(u3, e_ref[:, cols]))

    w_step(3)
    for h in range(2):
        for stage in range(1, 5):
            xy_two(h, stage)
    yacc[...] = term(0)
    w_ready(0)
    product(1, -1)
    w_ready(1)
    product(2, -2)
    g_step(4)

    def coefficients(row):
        @pl.loop(0, 1024, step=TILE)
        def _(c):
            cols = pl.ds(pl.multiple_of(row * 1024 + c, TILE), TILE)
            cbuf[:, cols] += sum3(nn(v3, gbuf[:, cols]))

    for dy in (2, 1, 3):
        row = lax.rem(y + dy, YS)
        coefficients(row)
        for j in range(PLANE):
            r_copy(row * PLANE + j).start()
    coefficients(y)
    for k in ks_a:
        r_copy(a_to[k]).start()
    cin[dp] = cbuf[:, my_piece]
    w_step(4)
    w_ready(2)
    product(3, -3)
    w_ready(3)
    yb[...] = (yacc[...] + term(4)).astype(BF16)
    for k in range(XS * YS - 1):
        y_copy(k).start()
    out_ref[:, chip_cols] = yb[mine, :]
    settle(cin.at[pl.ds(0, DP - 1)], cf_recv.at[0])
    total = cin[0]
    for k in range(1, DP):
        total += cin[k]
    coef_ref[:, my_piece] = total * (1.0 / 32)
    for k in range(DP - 1):
        s_copy(k).start()
    merge(0, 4096)
    settle(coef_ref.at[:, pl.ds(0, 128 * (DP - 1))], cf_recv.at[1])
    settle(cbuf.at[:, pl.ds(0, 128 * (DP - 1))], cf_send.at[0])
    settle(coef_ref.at[:, pl.ds(0, 128 * (DP - 1))], cf_send.at[1])
    settle(abuf.at[pl.ds(0, PLANE - 1)], sk_send.at[0])
    settle(bbuf.at[pl.ds(0, YS - 1)], sk_send.at[1])
    settle(xa.at[pl.ds(0, 32), pl.ds(0, 3584)], xz_send)
    settle(wz.at[0, 0, 0, pl.ds(0, 56)], c_send)
    settle(tdst.at[pl.ds(0, 7)], t_send)
    settle(wz.at[0], k_send)
    for h in range(2):
        settle(wz.at[0, 0, pl.ds(0, 3), pl.ds(0, 32)], p_send.at[h, 0])
        settle(wz.at[0, pl.ds(0, 3), :, pl.ds(0, 32)], p_send.at[h, 1])
    settle(gbuf.at[pl.ds(0, 224)], g_send)
    settle(wp.at[0, pl.ds(0, 3584)], w_send)
    settle(wp.at[0, pl.ds(0, 3584)], wc_send)
    settle(xa.at[pl.ds(0, 480)], xy_send)
    settle(yb.at[pl.ds(0, 480)], y_recv)
    settle(yb.at[pl.ds(0, 480)], y_send)


def error_kernel(m_ref, u_ref, c_ref, y_ref, o_hbm, out_hbm, coef_hbm, basis_hbm, o_ref, basis_ref, sem, o_sem):
    basis_ref[...] = u_ref[...] * math.sqrt(512)
    through = [pltpu.make_async_copy(a, b, sem.at[i]) for i, (a, b) in enumerate(
        ((y_ref, out_hbm), (c_ref, coef_hbm), (basis_ref, basis_hbm)))]
    for c in through:
        c.start()
    u0, u1, u2 = pieces(u_ref[...])
    left = jnp.concatenate([u0, u0, u1, u0, u2, u1], axis=0).T.astype(BF16)
    width = 4096 // PARTS
    stores = []
    for i in range(PARTS):
        cols = pl.ds(i * width, width)
        c0, c1, c2 = pieces(c_ref[:, cols])
        right = jnp.concatenate([c0, c1, c0, c2, c0, c1], axis=0).astype(BF16)
        for r in range(0, 512, 256):
            for c in range(0, width, 256):
                at = (slice(r, r + 256), pl.ds(i * width + c, 256))
                o_ref[at] = (m_ref[at] - nn(left[r : r + 256], right[:, c : c + 256])).astype(BF16)
        stores.append(pltpu.make_async_copy(o_ref.at[:, cols], o_hbm.at[:, cols], o_sem.at[i]))
        stores[i].start()
    for c in stores + through:
        c.wait()


def shards(inputs, weight, out_grad, error_feedback, warm_coeffs):
    S = jax.ShapeDtypeStruct
    V = pl.BlockSpec(memory_space=pltpu.VMEM)
    A = pl.BlockSpec(memory_space=pl.ANY)
    D = pltpu.SemaphoreType.DMA
    VM = pltpu.VMEM
    hbm = lambda v: pltpu.with_memory_space_constraint(v, pltpu.HBM)
    operands = [hbm(v) for v in (inputs, weight, out_grad, error_feedback[0], warm_coeffs[0])]
    out, coef, merged, unit = pl.pallas_call(
        main_kernel,
        out_shape=(VM((32, 4096), BF16), VM((8, 4096), F32), VM((512, 4096), F32), VM((8, 512), F32)),
        in_specs=[A, A, A, A, A],
        out_specs=(V, V, V, V),
        scratch_shapes=[
            VM((256, 512), BF16),
            VM((512, 4096), BF16),
            VM((256, 4096), BF16),
            VM((512, 4096), BF16),
            VM((CORES, 4096, 128), BF16),
            VM((512, 256), F32),
            VM((512, 256), BF16),
            VM((8, 4096), F32),
            VM((CORES, YS, XS, 64, 128), F32),
            VM((192, 4096), BF16),
            VM((128, 4096), BF16),
            VM((8, 8, 128), F32),
            VM((8, 8, 128), F32),
            VM((24, 512), F32),
            VM((512, 256), BF16),
            VM((8, 4096), F32),
            VM((PLANE, 8, 512), F32),
            VM((YS, 8, 512), F32),
            VM((DP, 8, 128), F32),
            VM((2, 8, 512), F32),
            D((7,)),
            D, D((2, 2, 4)),
            D, D((2,)),
            D, D((2, 5, 2)),
            D, D((2, 2, 4)),
            D, D((4,)),
            D, D,
            D((2,)), D((2,)),
            D((2,)), D((2,)),
            D, D,
            D((2, 2)), D((2, 2)),
            D, D,
            D, D,
        ],
        compiler_params=pltpu.CompilerParams(
            collective_id=0, has_side_effects=True, vmem_limit_bytes=40 * 2**20),
    )(*operands)
    err, out, coef, basis = pl.pallas_call(
        error_kernel,
        out_shape=(S((512, 4096), BF16), S((32, 4096), BF16), S((8, 4096), F32), S((8, 512), F32)),
        in_specs=[V, V, V, V],
        out_specs=(A, A, A, A),
        scratch_shapes=[VM((512, 4096), BF16), VM((8, 512), F32), D((3,)), D((PARTS,))],
        compiler_params=pltpu.CompilerParams(vmem_limit_bytes=24 * 2**20),
    )(merged, unit, coef, out)
    return (out, basis, coef[None], err[None])


def solution(mesh):
    in_specs = (
        P("dp", "tensor"),
        P("tensor", None),
        P(("dp", "tensor"), None),
        P("dp", "tensor", None),
        P("tensor", None, None),
    )
    out_specs = (
        P(("dp", "tensor"), None),
        P(None, "tensor"),
        P("tensor", None, None),
        P("dp", "tensor", None),
    )
    return jax.shard_map(shards, mesh=mesh, in_specs=in_specs, out_specs=out_specs, check_vma=False)
```

```python
import functools
import math

import jax
import jax.numpy as jnp
from jax import lax
from jax.experimental import pallas as pl
from jax.experimental.pallas import tpu as pltpu
from jax.sharding import PartitionSpec as P

MESH = pl.DeviceIdType.MESH
F32 = jnp.float32
BF16 = jnp.bfloat16
EPSILON = 1e-06
TILE = 512
PARTS = 8
SLOTS = (0, -1, 1, 2, -2, 3, -3, 4)
XS, YS, CORES = 4, 4, 2
PLANE = XS * CORES
DP = YS * PLANE
OFFSETS = sorted(
    ((dy, dx, dc) for dy in range(YS) for dx in range(XS) for dc in range(CORES)),
    key=lambda o: (-min(o[0], YS - o[0]) - min(o[1], XS - o[1]), -o[2]))


def nn(a, b):
    return lax.dot_general(a, b, (((1,), (0,)), ((), ())), preferred_element_type=F32)


def nt(a, b):
    return lax.dot_general(a, b, (((1,), (1,)), ((), ())), preferred_element_type=F32)


def pieces(v):
    high = v.astype(BF16).astype(F32)
    rest = v - high
    middle = rest.astype(BF16).astype(F32)
    return high, middle, rest - middle


def split3(v):
    return jnp.concatenate(pieces(v), axis=0).astype(BF16)


def sum3(v):
    n = v.shape[0] // 3
    return v[:n] + v[n : 2 * n] + v[2 * n :]


def orthonormal(v):
    rows = lax.broadcasted_iota(jnp.int32, (v.shape[0], 1), 0)
    for i in range(v.shape[0]):
        row = v[i : i + 1]
        dots = jnp.sum(v * row, axis=1, keepdims=True)
        scale = lax.rsqrt(dots[i : i + 1] + EPSILON)
        unit = row * scale
        v = jnp.where(rows == i, unit, jnp.where(rows > i, v - (dots * scale) * unit, v))
    return v


def main_kernel(
    x_hbm, w_hbm, g_hbm, e_hbm, wc_hbm,
    out_ref, coef_ref, merged_ref, u_ref,
    x_ref, e_ref, gbuf, xa, wp, yacc, yb, wc_ref, wz, w3_ref, gpad, tsrc, tdst, se_ref, xt_ref, cbuf,
    abuf, bbuf, cin, sk_src,
    lsem, g_send, g_recv, xz_send, xz_recv, xy_send, xy_recv, w_send, w_recv, wc_send, wc_recv,
    y_send, y_recv, sk_send, sk_recv, cf_send, cf_recv, c_send, c_recv, p_send, p_recv, k_send, k_recv,
    t_send, t_recv,
):
    n = 8
    me = lax.axis_index("tensor")
    dp = lax.axis_index("dp")
    core = dp % CORES
    chip = dp // CORES
    y, xc = dp // PLANE, dp % PLANE
    xq = xc // CORES
    z_all = [lax.rem(me + k, n) for k in range(n)]
    z_to = [z_all[1], z_all[n - 1]]
    sign = (1, -1)
    a_to = [y * PLANE + lax.rem(xc + k, PLANE) for k in range(PLANE)]
    b_to = [lax.rem(y + k, YS) * PLANE + xc for k in range(YS)]
    d_to = [lax.rem(y + dy, YS) * PLANE + lax.rem(xq + dx, XS) * CORES + lax.rem(core + dc, CORES) for dy, dx, dc in OFFSETS]
    chips = [lax.rem(y + dy, YS) * XS + lax.rem(xq + dx, XS) for dy, dx, dc in OFFSETS if dc == 0]
    p_to = [c * CORES + core for c in chips]
    partner = chip * CORES + (1 - core)

    def shifted(axis, r):
        if axis == 0:
            return y * XS + lax.rem(xq + r + XS, XS)
        return lax.rem(y + r + YS, YS) * XS + xq

    own = pl.ds(pl.multiple_of(me * 32, 32), 32)
    mine = pl.ds(pl.multiple_of(chip * 32, 32), 32)
    own_cols = pl.ds(pl.multiple_of(me * 512, 512), 512)
    own_rows = own_cols
    chip_cols = pl.ds(pl.multiple_of(chip * 256, 256), 256)
    lx = pltpu.make_async_copy(x_hbm, x_ref, lsem.at[0])
    lw = [pltpu.make_async_copy(
        w_hbm.at[:, pl.ds(pl.multiple_of(chip * 256 + c * 128, 128), 128)], wp.at[c, own_rows], lsem.at[1 + 5 * c])
        for c in range(CORES)]
    le = pltpu.make_async_copy(e_hbm, e_ref, lsem.at[2])
    lg = pltpu.make_async_copy(g_hbm, gbuf.at[own], lsem.at[3])
    lc = pltpu.make_async_copy(wc_hbm, wc_ref, lsem.at[5])
    lp = pltpu.make_async_copy(g_hbm, gpad.at[pl.ds(pl.multiple_of(lax.rem(me, 4) * 32, 32), 32)], lsem.at[4])
    for c in (lc, lx, lg, le, *lw):
        c.start()

    barrier = pltpu.get_barrier_semaphore()
    for z in z_all[1:]:
        pl.semaphore_signal(barrier, inc=1, device_id={"tensor": z}, device_id_type=MESH)
    near = [y * PLANE + lax.rem(xq + k, XS) * CORES + core for k in range(1, XS)] + b_to[1:] + [partner]
    for d in near:
        pl.semaphore_signal(barrier, inc=1, device_id={"dp": d}, device_id_type=MESH)
    gpad[...] = jnp.zeros_like(gpad)
    lp.start()
    pl.semaphore_wait(barrier, 7 + 3 + 3 + 1)

    def settle(ref, sem):
        pltpu.make_async_copy(ref, ref, sem).wait()

    def steps(d, h):
        return 4 if d == h else 3

    def ring_copy(buf, rows, part, send, recv, d, h, s):
        block = lax.rem(me - sign[d] * s + n, n)
        at = pl.ds(pl.multiple_of(block * rows + h * part, part), part)
        return pltpu.make_async_remote_copy(
            src_ref=buf.at[at], dst_ref=buf.at[at],
            send_sem=send, recv_sem=recv.at[d, h, s],
            device_id={"tensor": z_to[d]}, device_id_type=MESH)

    def g_copy(d, h, s):
        return ring_copy(gbuf, 32, 16, g_send, g_recv, d, h, s)

    def w_copy(d, h, s):
        return ring_copy(wp.at[core], 512, 256, w_send, w_recv, d, h, s)

    def wc_copy(d, h, s):
        block = lax.rem(me - sign[d] * (s + 1) + n, n)
        at = pl.ds(pl.multiple_of(block * 512 + h * 256, 256), 256)
        return pltpu.make_async_remote_copy(
            src_ref=wp.at[core, at], dst_ref=wp.at[core, at],
            send_sem=wc_send, recv_sem=wc_recv.at[s],
            device_id={"dp": partner}, device_id_type=MESH)

    def g_step(s):
        for h in range(2):
            for d in range(2):
                if s > 0 and s - 1 < steps(d, h):
                    g_copy(d, h, s - 1).wait_recv()
                if s < steps(d, h):
                    g_copy(d, h, s).start()

    def w_step(s):
        for h in range(2):
            for d in range(2):
                if s > 0 and s - 1 < steps(d, h):
                    w_copy(d, h, s - 1).wait_recv()
                if s < steps(d, h):
                    w_copy(d, h, s).start()
                if s > 0 and s - 1 < steps(d, h):
                    wc_copy(d, h, s - 1).start()

    def slot_cols(shift):
        return pl.ds(SLOTS.index(shift) * 512, 512)

    def xz_copy(k):
        src = pl.ds(pl.multiple_of(lax.rem(me + k + n, n) * 32, 32), 32)
        there = 4 if k == 4 else -k
        return pltpu.make_async_remote_copy(
            src_ref=x_ref.at[src], dst_ref=xa.at[mine, slot_cols(there)],
            send_sem=xz_send, recv_sem=xz_recv.at[SLOTS.index(there) // 4],
            device_id={"tensor": lax.rem(me + k + n, n)}, device_id_type=MESH)

    shifts = (0, -1, 1, 2)

    def xy_copy(h, stage, kind):
        first = h
        second = 1 - h
        axis = first if stage == 0 else second
        r = 0 if stage == 0 else shifts[stage - 1]
        b = (0, 0, -1, 1)[kind]
        go = (1, -1, 1, -1)[kind]
        ra, rb = (b, 0) if stage == 0 else (r, b)
        if first == 0:
            rx, ry = ra, rb
        else:
            rx, ry = rb, ra
        block = lax.rem(y + ry + YS, YS) * XS + lax.rem(xq + rx + XS, XS)
        at = pl.ds(pl.multiple_of(block * 32 + (16 if kind == 3 else 0), 16), 32 if kind < 2 else 16)
        cols = pl.ds(h * 2048, 2048)
        return pltpu.make_async_remote_copy(
            src_ref=xa.at[at, cols], dst_ref=xa.at[at, cols],
            send_sem=xy_send, recv_sem=xy_recv.at[h, stage, kind // 2],
            device_id={"dp": shifted(axis, go) * CORES + core}, device_id_type=MESH)

    def xy_full(h, stage):
        xy_copy(h, stage, 0).start()
        xy_copy(h, stage, 1).start()

    def xy_one(h, stage):
        settle(xa.at[pl.ds(0, 64), pl.ds(0, 2048)], xy_recv.at[h, stage, 0])
        xy_copy(h, stage, 2).start()
        xy_copy(h, stage, 3).start()

    def xy_two(h, stage):
        settle(xa.at[pl.ds(0, 32), pl.ds(0, 2048)], xy_recv.at[h, stage, 1])
        if stage == 0:
            xy_full(h, 4)

    def y_copy(k):
        src = pl.ds(pl.multiple_of(chips[k] * 32, 32), 32)
        return pltpu.make_async_remote_copy(
            src_ref=yb.at[src], dst_ref=out_ref.at[:, chip_cols],
            send_sem=y_send, recv_sem=y_recv,
            device_id={"dp": p_to[k]}, device_id_type=MESH)

    def c_copy(k):
        return pltpu.make_async_remote_copy(
            src_ref=wc_ref.at[:, pl.ds(pl.multiple_of(dp * 128, 128), 128)],
            dst_ref=wz.at[core, y, xq, pl.ds(pl.multiple_of(me * 8, 8), 8)],
            send_sem=c_send, recv_sem=c_recv,
            device_id={"tensor": z_all[k]}, device_id_type=MESH)

    def p_copy(h, phase, k):
        rows = pl.ds(h * 32, 32)
        axis = h if phase == 0 else 1 - h
        if phase == 0:
            at = wz.at[core, y, xq, rows]
        elif axis == 1:
            at = wz.at[core, y, :, rows]
        else:
            at = wz.at[core, :, xq, rows]
        return pltpu.make_async_remote_copy(
            src_ref=at, dst_ref=at, send_sem=p_send.at[h, phase], recv_sem=p_recv.at[h, phase],
            device_id={"dp": shifted(axis, k) * CORES + core}, device_id_type=MESH)

    def k_copy(h):
        at = wz.at[core, :, :, pl.ds(h * 32, 32)]
        return pltpu.make_async_remote_copy(
            src_ref=at, dst_ref=at, send_sem=k_send, recv_sem=k_recv,
            device_id={"dp": partner}, device_id_type=MESH)

    def t_copy(k):
        return pltpu.make_async_remote_copy(
            src_ref=tsrc.at[z_all[k]], dst_ref=tdst.at[me], send_sem=t_send, recv_sem=t_recv,
            device_id={"tensor": z_all[k]}, device_id_type=MESH)

    def a_copy(k, src, dst, send, recv):
        return pltpu.make_async_remote_copy(
            src_ref=src, dst_ref=dst, send_sem=send.at[0], recv_sem=recv.at[0],
            device_id={"dp": a_to[k]}, device_id_type=MESH)

    def b_copy(k, src, dst, send, recv):
        return pltpu.make_async_remote_copy(
            src_ref=src, dst_ref=dst, send_sem=send.at[1], recv_sem=recv.at[1],
            device_id={"dp": b_to[k]}, device_id_type=MESH)

    def merge(low, high):
        @pl.loop(low, high, step=TILE)
        def _(c):
            cols = pl.ds(pl.multiple_of(c, TILE), TILE)
            merged_ref[:, cols] = e_ref[:, cols].astype(F32) + nn(xt_ref[...], gbuf[:, cols])

    def term(shift):
        t = lax.rem(me + shift + n, n)
        at = pl.ds(pl.multiple_of(t * 512, 512), 512)
        return nn(xa[:, slot_cols(shift)], jnp.concatenate([wp[0, at], wp[1, at]], axis=1))

    def product(*shifts):
        yacc[...] += sum(term(shift) for shift in shifts)

    def w_ready(s):
        settle(wp.at[0, pl.ds(0, 1024 if s < 3 else 512)], wc_recv.at[s])

    def piece(j):
        return pl.ds(pl.multiple_of(j * 128, 128), 128)

    my_piece = piece(dp)

    def r_copy(to):
        return pltpu.make_async_remote_copy(
            src_ref=cbuf.at[:, piece(to)], dst_ref=cin.at[dp],
            send_sem=cf_send.at[0], recv_sem=cf_recv.at[0],
            device_id={"dp": to}, device_id_type=MESH)

    def s_copy(k):
        return pltpu.make_async_remote_copy(
            src_ref=coef_ref.at[:, my_piece], dst_ref=coef_ref.at[:, my_piece],
            send_sem=cf_send.at[1], recv_sem=cf_recv.at[1],
            device_id={"dp": d_to[k]}, device_id_type=MESH)

    lc.wait()
    for k in range(1, n):
        c_copy(k).start()
    wz[core, y, xq, pl.ds(pl.multiple_of(me * 8, 8), 8)] = wc_ref[:, pl.ds(pl.multiple_of(dp * 128, 128), 128)]
    lx.wait()
    for k in (1, -1, -2, 2, -3, 3, 4):
        xz_copy(k).start()
    lg.wait()
    g_step(0)
    for c in lw:
        c.wait()
    w_step(0)
    xa[mine, slot_cols(0)] = x_ref[own, :]
    xt_ref[...] = x_ref[...].T
    settle(wz.at[0, 0, 0, pl.ds(0, 56)], c_recv)
    for h in range(2):
        for k in range(1, 4):
            p_copy(h, 0, k).start()
    settle(xa.at[pl.ds(0, 32), pl.ds(0, 1536)], xz_recv.at[0])
    xy_full(0, 0)
    xy_full(0, 1)
    le.wait()
    se_ref[...] = jnp.zeros_like(se_ref)

    def sketch_error(low, high):
        @pl.loop(low, high, step=TILE)
        def _(c):
            cols = pl.ds(pl.multiple_of(c, TILE), TILE)
            se_ref[...] += nt(split3(wc_ref[:, cols]), e_ref[:, cols])

    sketch_error(0, 2048)
    for h in range(2):
        settle(wz.at[0, 0, pl.ds(0, 3), pl.ds(0, 32)], p_recv.at[h, 0])
        for k in range(1, 4):
            p_copy(h, 1, k).start()
    settle(xa.at[pl.ds(0, 32), pl.ds(0, 2048)], xz_recv.at[1])
    xy_full(1, 0)
    xy_full(1, 1)
    xy_one(0, 0)
    xy_full(0, 2)
    xy_one(0, 1)
    sketch_error(2048, 4096)
    g_step(1)
    for h in range(2):
        settle(wz.at[0, pl.ds(0, 3), :, pl.ds(0, 32)], p_recv.at[h, 1])
        k_copy(h).start()
    settle(wz.at[0], k_recv)
    for d in range(DP):
        w3_ref[:, d * 128 : d * 128 + 128] = split3(wz[d % CORES, d // PLANE, d % PLANE // CORES])
    lp.wait()
    partial = sum3(nt(w3_ref[...], gpad[...]))
    for t in range(n):
        tsrc[t] = partial[t * 8 : t * 8 + 8]
    for k in range(1, n):
        t_copy(k).start()
    tdst[me] = tsrc[me]
    xy_one(1, 0)
    xy_full(1, 2)
    xy_full(0, 3)
    xy_full(1, 3)
    w_step(1)
    xy_two(0, 0)
    xy_one(1, 1)
    g_step(2)
    settle(tdst.at[pl.ds(0, 7)], t_recv)
    tokens = jnp.concatenate(
        [tdst[0] + tdst[1] + tdst[2] + tdst[3], tdst[4] + tdst[5] + tdst[6] + tdst[7]], axis=1)
    sketch = sum3(se_ref[...]) + sum3(nn(split3(tokens), x_ref[...]))
    ks_a, ks_b = range(1, PLANE), range(1, YS)
    sk_src[0] = sketch
    for k in ks_a:
        a_copy(k, sk_src.at[0], abuf.at[xc], sk_send, sk_recv).start()
    abuf[xc] = sketch
    xy_two(1, 0)
    xy_one(0, 2)
    xy_one(1, 2)
    w_step(2)
    settle(abuf.at[pl.ds(0, PLANE - 1)], sk_recv.at[0])
    total = abuf[0]
    for k in range(1, PLANE):
        total += abuf[k]
    sk_src[1] = total
    for k in ks_b:
        b_copy(k, sk_src.at[1], bbuf.at[y], sk_send, sk_recv).start()
    bbuf[y] = total
    g_step(3)
    xy_one(0, 3)
    xy_one(1, 3)
    xy_one(0, 4)
    xy_one(1, 4)
    settle(bbuf.at[pl.ds(0, YS - 1)], sk_recv.at[1])
    total = bbuf[0]
    for k in range(1, YS):
        total += bbuf[k]
    unit = orthonormal(total)
    u_ref[...] = unit
    u3 = split3(unit)
    v3 = split3(sum3(nt(u3, x_ref[...])))
    w_step(3)

    @pl.loop(0, 4096, step=TILE)
    def _(c):
        cols = pl.ds(pl.multiple_of(c, TILE), TILE)
        cbuf[:, cols] = sum3(nn(u3, e_ref[:, cols]))

    g_step(4)

    def coefficients(row):
        @pl.loop(0, 1024, step=TILE)
        def _(c):
            cols = pl.ds(pl.multiple_of(row * 1024 + c, TILE), TILE)
            cbuf[:, cols] += sum3(nn(v3, gbuf[:, cols]))

    for dy in (2, 1, 3):
        row = lax.rem(y + dy, YS)
        coefficients(row)
        for j in range(PLANE):
            r_copy(row * PLANE + j).start()
    coefficients(y)
    for k in ks_a:
        r_copy(a_to[k]).start()
    cin[dp] = cbuf[:, my_piece]
    w_step(4)
    for h in range(2):
        for stage in range(1, 5):
            xy_two(h, stage)
    yacc[...] = term(0)
    w_ready(0)
    product(1, -1)
    w_ready(1)
    product(2, -2)
    w_ready(2)
    product(3, -3)
    w_ready(3)
    yb[...] = (yacc[...] + term(4)).astype(BF16)
    for k in range(XS * YS - 1):
        y_copy(k).start()
    out_ref[:, chip_cols] = yb[mine, :]
    settle(cin.at[pl.ds(0, DP - 1)], cf_recv.at[0])
    total = cin[0]
    for k in range(1, DP):
        total += cin[k]
    coef_ref[:, my_piece] = total * (1.0 / 32)
    for k in range(DP - 1):
        s_copy(k).start()
    merge(0, 4096)
    settle(coef_ref.at[:, pl.ds(0, 128 * (DP - 1))], cf_recv.at[1])
    settle(cbuf.at[:, pl.ds(0, 128 * (DP - 1))], cf_send.at[0])
    settle(coef_ref.at[:, pl.ds(0, 128 * (DP - 1))], cf_send.at[1])
    settle(abuf.at[pl.ds(0, PLANE - 1)], sk_send.at[0])
    settle(bbuf.at[pl.ds(0, YS - 1)], sk_send.at[1])
    settle(xa.at[pl.ds(0, 32), pl.ds(0, 3584)], xz_send)
    settle(wz.at[0, 0, 0, pl.ds(0, 56)], c_send)
    settle(tdst.at[pl.ds(0, 7)], t_send)
    settle(wz.at[0], k_send)
    for h in range(2):
        settle(wz.at[0, 0, pl.ds(0, 3), pl.ds(0, 32)], p_send.at[h, 0])
        settle(wz.at[0, pl.ds(0, 3), :, pl.ds(0, 32)], p_send.at[h, 1])
    settle(gbuf.at[pl.ds(0, 224)], g_send)
    settle(wp.at[0, pl.ds(0, 3584)], w_send)
    settle(wp.at[0, pl.ds(0, 3584)], wc_send)
    settle(xa.at[pl.ds(0, 480)], xy_send)
    settle(yb.at[pl.ds(0, 480)], y_recv)
    settle(yb.at[pl.ds(0, 480)], y_send)


def error_kernel(m_ref, u_ref, c_ref, y_ref, o_hbm, out_hbm, coef_hbm, basis_hbm, o_ref, basis_ref, sem, o_sem):
    basis_ref[...] = u_ref[...] * math.sqrt(512)
    through = [pltpu.make_async_copy(a, b, sem.at[i]) for i, (a, b) in enumerate(
        ((y_ref, out_hbm), (c_ref, coef_hbm), (basis_ref, basis_hbm)))]
    for c in through:
        c.start()
    u0, u1, u2 = pieces(u_ref[...])
    left = jnp.concatenate([u0, u0, u1, u0, u2, u1], axis=0).T.astype(BF16)
    width = 4096 // PARTS
    stores = []
    for i in range(PARTS):
        cols = pl.ds(i * width, width)
        c0, c1, c2 = pieces(c_ref[:, cols])
        right = jnp.concatenate([c0, c1, c0, c2, c0, c1], axis=0).astype(BF16)
        for r in range(0, 512, 256):
            for c in range(0, width, 256):
                at = (slice(r, r + 256), pl.ds(i * width + c, 256))
                o_ref[at] = (m_ref[at] - nn(left[r : r + 256], right[:, c : c + 256])).astype(BF16)
        stores.append(pltpu.make_async_copy(o_ref.at[:, cols], o_hbm.at[:, cols], o_sem.at[i]))
        stores[i].start()
    for c in stores + through:
        c.wait()


def shards(inputs, weight, out_grad, error_feedback, warm_coeffs):
    S = jax.ShapeDtypeStruct
    V = pl.BlockSpec(memory_space=pltpu.VMEM)
    A = pl.BlockSpec(memory_space=pl.ANY)
    D = pltpu.SemaphoreType.DMA
    VM = pltpu.VMEM
    hbm = lambda v: pltpu.with_memory_space_constraint(v, pltpu.HBM)
    operands = [hbm(v) for v in (inputs, weight, out_grad, error_feedback[0], warm_coeffs[0])]
    out, coef, merged, unit = pl.pallas_call(
        main_kernel,
        out_shape=(VM((32, 4096), BF16), VM((8, 4096), F32), VM((512, 4096), F32), VM((8, 512), F32)),
        in_specs=[A, A, A, A, A],
        out_specs=(V, V, V, V),
        scratch_shapes=[
            VM((256, 512), BF16),
            VM((512, 4096), BF16),
            VM((256, 4096), BF16),
            VM((512, 4096), BF16),
            VM((CORES, 4096, 128), BF16),
            VM((512, 256), F32),
            VM((512, 256), BF16),
            VM((8, 4096), F32),
            VM((CORES, YS, XS, 64, 128), F32),
            VM((192, 4096), BF16),
            VM((128, 4096), BF16),
            VM((8, 8, 128), F32),
            VM((8, 8, 128), F32),
            VM((24, 512), F32),
            VM((512, 256), BF16),
            VM((8, 4096), F32),
            VM((PLANE, 8, 512), F32),
            VM((YS, 8, 512), F32),
            VM((DP, 8, 128), F32),
            VM((2, 8, 512), F32),
            D((7,)),
            D, D((2, 2, 4)),
            D, D((2,)),
            D, D((2, 5, 2)),
            D, D((2, 2, 4)),
            D, D((4,)),
            D, D,
            D((2,)), D((2,)),
            D((2,)), D((2,)),
            D, D,
            D((2, 2)), D((2, 2)),
            D, D,
            D, D,
        ],
        compiler_params=pltpu.CompilerParams(
            collective_id=0, has_side_effects=True, vmem_limit_bytes=40 * 2**20),
    )(*operands)
    err, out, coef, basis = pl.pallas_call(
        error_kernel,
        out_shape=(S((512, 4096), BF16), S((32, 4096), BF16), S((8, 4096), F32), S((8, 512), F32)),
        in_specs=[V, V, V, V],
        out_specs=(A, A, A, A),
        scratch_shapes=[VM((512, 4096), BF16), VM((8, 512), F32), D((3,)), D((PARTS,))],
        compiler_params=pltpu.CompilerParams(vmem_limit_bytes=24 * 2**20),
    )(merged, unit, coef, out)
    return (out, basis, coef[None], err[None])


def solution(mesh):
    in_specs = (
        P("dp", "tensor"),
        P("tensor", None),
        P(("dp", "tensor"), None),
        P("dp", "tensor", None),
        P("tensor", None, None),
    )
    out_specs = (
        P(("dp", "tensor"), None),
        P(None, "tensor"),
        P("tensor", None, None),
        P("dp", "tensor", None),
    )
    return jax.shard_map(shards, mesh=mesh, in_specs=in_specs, out_specs=out_specs, check_vma=False)
```

```python
import functools
import math

import jax
import jax.numpy as jnp
from jax import lax
from jax.experimental import pallas as pl
from jax.experimental.pallas import tpu as pltpu
from jax.sharding import PartitionSpec as P

MESH = pl.DeviceIdType.MESH
F32 = jnp.float32
BF16 = jnp.bfloat16
EPSILON = 1e-06
TILE = 512
PARTS = 8
SLOTS = (0, -1, 1, 2, -2, 3, -3, 4)
XS, YS, CORES = 4, 4, 2
PLANE = XS * CORES
DP = YS * PLANE
OFFSETS = sorted(
    ((dy, dx, dc) for dy in range(YS) for dx in range(XS) for dc in range(CORES)),
    key=lambda o: (-min(o[0], YS - o[0]) - min(o[1], XS - o[1]), -o[2]))


def nn(a, b):
    return lax.dot_general(a, b, (((1,), (0,)), ((), ())), preferred_element_type=F32)


def nt(a, b):
    return lax.dot_general(a, b, (((1,), (1,)), ((), ())), preferred_element_type=F32)


def pieces(v):
    high = v.astype(BF16).astype(F32)
    rest = v - high
    middle = rest.astype(BF16).astype(F32)
    return high, middle, rest - middle


def split3(v):
    return jnp.concatenate(pieces(v), axis=0).astype(BF16)


def sum3(v):
    n = v.shape[0] // 3
    return v[:n] + v[n : 2 * n] + v[2 * n :]


def orthonormal(v):
    rows = lax.broadcasted_iota(jnp.int32, (v.shape[0], 1), 0)
    for i in range(v.shape[0]):
        row = v[i : i + 1]
        dots = jnp.sum(v * row, axis=1, keepdims=True)
        scale = lax.rsqrt(dots[i : i + 1] + EPSILON)
        unit = row * scale
        v = jnp.where(rows == i, unit, jnp.where(rows > i, v - (dots * scale) * unit, v))
    return v


def main_kernel(
    x_hbm, w_hbm, g_hbm, e_hbm, wc_hbm,
    out_ref, coef_ref, merged_ref, u_ref,
    x_ref, e_ref, gbuf, xa, wp, yacc, yb, wc_ref, wz, w3_ref, gpad, tsrc, tdst, se_ref, xt_ref, xg_ref, cbuf,
    abuf, bbuf, cin, sk_src,
    lsem, g_send, g_recv, xz_send, xz_recv, xy_send, xy_recv, w_send, w_recv, wc_send, wc_recv,
    y_send, y_recv, sk_send, sk_recv, cf_send, cf_recv, c_send, c_recv, p_send, p_recv, k_send, k_recv,
    t_send, t_recv,
):
    n = 8
    me = lax.axis_index("tensor")
    dp = lax.axis_index("dp")
    core = dp % CORES
    chip = dp // CORES
    y, xc = dp // PLANE, dp % PLANE
    xq = xc // CORES
    z_all = [lax.rem(me + k, n) for k in range(n)]
    z_to = [z_all[1], z_all[n - 1]]
    sign = (1, -1)
    a_to = [y * PLANE + lax.rem(xc + k, PLANE) for k in range(PLANE)]
    b_to = [lax.rem(y + k, YS) * PLANE + xc for k in range(YS)]
    d_to = [lax.rem(y + dy, YS) * PLANE + lax.rem(xq + dx, XS) * CORES + lax.rem(core + dc, CORES) for dy, dx, dc in OFFSETS]
    chips = [lax.rem(y + dy, YS) * XS + lax.rem(xq + dx, XS) for dy, dx, dc in OFFSETS if dc == 0]
    p_to = [c * CORES + core for c in chips]
    partner = chip * CORES + (1 - core)

    def shifted(axis, r):
        if axis == 0:
            return y * XS + lax.rem(xq + r + XS, XS)
        return lax.rem(y + r + YS, YS) * XS + xq

    own = pl.ds(pl.multiple_of(me * 32, 32), 32)
    mine = pl.ds(pl.multiple_of(chip * 32, 32), 32)
    own_cols = pl.ds(pl.multiple_of(me * 512, 512), 512)
    own_rows = own_cols
    chip_cols = pl.ds(pl.multiple_of(chip * 256, 256), 256)
    lx = pltpu.make_async_copy(x_hbm, x_ref, lsem.at[0])
    lw = [pltpu.make_async_copy(
        w_hbm.at[:, pl.ds(pl.multiple_of(chip * 256 + c * 128, 128), 128)], wp.at[c, own_rows], lsem.at[1 + 5 * c])
        for c in range(CORES)]
    le = pltpu.make_async_copy(e_hbm, e_ref, lsem.at[2])
    lg = pltpu.make_async_copy(g_hbm, gbuf.at[pl.ds(0, 32)], lsem.at[3])
    lc = pltpu.make_async_copy(wc_hbm, wc_ref, lsem.at[5])
    lp = pltpu.make_async_copy(g_hbm, gpad.at[pl.ds(pl.multiple_of(lax.rem(me, 4) * 32, 32), 32)], lsem.at[4])
    for c in (lc, lx, lg, le, *lw):
        c.start()

    barrier = pltpu.get_barrier_semaphore()
    for z in z_all[1:]:
        pl.semaphore_signal(barrier, inc=1, device_id={"tensor": z}, device_id_type=MESH)
    near = [y * PLANE + lax.rem(xq + k, XS) * CORES + core for k in range(1, XS)] + b_to[1:] + [partner]
    for d in near:
        pl.semaphore_signal(barrier, inc=1, device_id={"dp": d}, device_id_type=MESH)
    gpad[...] = jnp.zeros_like(gpad)
    lp.start()
    pl.semaphore_wait(barrier, 7 + 3 + 3 + 1)

    def settle(ref, sem):
        pltpu.make_async_copy(ref, ref, sem).wait()

    def steps(d, h):
        return 4 if d == h else 3

    def ring_copy(buf, rows, part, send, recv, d, h, s):
        block = lax.rem(me - sign[d] * s + n, n)
        at = pl.ds(pl.multiple_of(block * rows + h * part, part), part)
        return pltpu.make_async_remote_copy(
            src_ref=buf.at[at], dst_ref=buf.at[at],
            send_sem=send, recv_sem=recv.at[d, h, s],
            device_id={"tensor": z_to[d]}, device_id_type=MESH)

    def g_copy(d, h, s):
        def at(shift):
            return gbuf.at[pl.ds(SLOTS.index(4 if abs(shift) == 4 else shift) * 32 + h * 16, 16)]

        return pltpu.make_async_remote_copy(
            src_ref=at(-sign[d] * s), dst_ref=at(-sign[d] * (s + 1)),
            send_sem=g_send, recv_sem=g_recv.at[d, h, s],
            device_id={"tensor": z_to[d]}, device_id_type=MESH)

    def w_copy(d, h, s):
        return ring_copy(wp.at[core], 512, 256, w_send, w_recv, d, h, s)

    def wc_copy(d, h, s):
        block = lax.rem(me - sign[d] * (s + 1) + n, n)
        at = pl.ds(pl.multiple_of(block * 512 + h * 256, 256), 256)
        return pltpu.make_async_remote_copy(
            src_ref=wp.at[core, at], dst_ref=wp.at[core, at],
            send_sem=wc_send, recv_sem=wc_recv.at[s],
            device_id={"dp": partner}, device_id_type=MESH)

    def g_step(s):
        for h in range(2):
            for d in range(2):
                if s > 0 and s - 1 < steps(d, h):
                    g_copy(d, h, s - 1).wait_recv()
                if s < steps(d, h):
                    g_copy(d, h, s).start()

    def w_step(s):
        for h in range(2):
            for d in range(2):
                if s > 0 and s - 1 < steps(d, h):
                    w_copy(d, h, s - 1).wait_recv()
                if s < steps(d, h):
                    w_copy(d, h, s).start()
                if s > 0 and s - 1 < steps(d, h):
                    wc_copy(d, h, s - 1).start()

    def slot_cols(shift):
        return pl.ds(SLOTS.index(shift) * 512, 512)

    def xz_copy(k):
        src = pl.ds(pl.multiple_of(lax.rem(me + k + n, n) * 32, 32), 32)
        there = 4 if k == 4 else -k
        return pltpu.make_async_remote_copy(
            src_ref=x_ref.at[src], dst_ref=xa.at[mine, slot_cols(there)],
            send_sem=xz_send, recv_sem=xz_recv.at[SLOTS.index(there) // 4],
            device_id={"tensor": lax.rem(me + k + n, n)}, device_id_type=MESH)

    shifts = (0, -1, 1, 2)

    def xy_copy(h, stage, kind):
        first = h
        second = 1 - h
        axis = first if stage == 0 else second
        r = 0 if stage == 0 else shifts[stage - 1]
        b = (0, 0, -1, 1)[kind]
        go = (1, -1, 1, -1)[kind]
        ra, rb = (b, 0) if stage == 0 else (r, b)
        if first == 0:
            rx, ry = ra, rb
        else:
            rx, ry = rb, ra
        block = lax.rem(y + ry + YS, YS) * XS + lax.rem(xq + rx + XS, XS)
        at = pl.ds(pl.multiple_of(block * 32 + (16 if kind == 3 else 0), 16), 32 if kind < 2 else 16)
        cols = pl.ds(h * 2048, 2048)
        return pltpu.make_async_remote_copy(
            src_ref=xa.at[at, cols], dst_ref=xa.at[at, cols],
            send_sem=xy_send, recv_sem=xy_recv.at[h, stage, kind // 2],
            device_id={"dp": shifted(axis, go) * CORES + core}, device_id_type=MESH)

    def xy_full(h, stage):
        xy_copy(h, stage, 0).start()
        xy_copy(h, stage, 1).start()

    def xy_one(h, stage):
        settle(xa.at[pl.ds(0, 64), pl.ds(0, 2048)], xy_recv.at[h, stage, 0])
        xy_copy(h, stage, 2).start()
        xy_copy(h, stage, 3).start()

    def xy_two(h, stage):
        settle(xa.at[pl.ds(0, 32), pl.ds(0, 2048)], xy_recv.at[h, stage, 1])
        if stage == 0:
            xy_full(h, 4)

    def y_copy(k):
        src = pl.ds(pl.multiple_of(chips[k] * 32, 32), 32)
        return pltpu.make_async_remote_copy(
            src_ref=yb.at[src], dst_ref=out_ref.at[:, chip_cols],
            send_sem=y_send, recv_sem=y_recv,
            device_id={"dp": p_to[k]}, device_id_type=MESH)

    def c_copy(k):
        return pltpu.make_async_remote_copy(
            src_ref=wc_ref.at[:, pl.ds(pl.multiple_of(dp * 128, 128), 128)],
            dst_ref=wz.at[core, y, xq, pl.ds(pl.multiple_of(me * 8, 8), 8)],
            send_sem=c_send, recv_sem=c_recv,
            device_id={"tensor": z_all[k]}, device_id_type=MESH)

    def p_copy(h, phase, k):
        rows = pl.ds(h * 32, 32)
        axis = h if phase == 0 else 1 - h
        if phase == 0:
            at = wz.at[core, y, xq, rows]
        elif axis == 1:
            at = wz.at[core, y, :, rows]
        else:
            at = wz.at[core, :, xq, rows]
        return pltpu.make_async_remote_copy(
            src_ref=at, dst_ref=at, send_sem=p_send.at[h, phase], recv_sem=p_recv.at[h, phase],
            device_id={"dp": shifted(axis, k) * CORES + core}, device_id_type=MESH)

    def k_copy(h):
        at = wz.at[core, :, :, pl.ds(h * 32, 32)]
        return pltpu.make_async_remote_copy(
            src_ref=at, dst_ref=at, send_sem=k_send, recv_sem=k_recv,
            device_id={"dp": partner}, device_id_type=MESH)

    def t_copy(k):
        return pltpu.make_async_remote_copy(
            src_ref=tsrc.at[z_all[k]], dst_ref=tdst.at[me], send_sem=t_send, recv_sem=t_recv,
            device_id={"tensor": z_all[k]}, device_id_type=MESH)

    def a_copy(k, src, dst, send, recv):
        return pltpu.make_async_remote_copy(
            src_ref=src, dst_ref=dst, send_sem=send.at[0], recv_sem=recv.at[0],
            device_id={"dp": a_to[k]}, device_id_type=MESH)

    def b_copy(k, src, dst, send, recv):
        return pltpu.make_async_remote_copy(
            src_ref=src, dst_ref=dst, send_sem=send.at[1], recv_sem=recv.at[1],
            device_id={"dp": b_to[k]}, device_id_type=MESH)

    def merge(low, high):
        @pl.loop(low, high, step=TILE)
        def _(c):
            cols = pl.ds(pl.multiple_of(c, TILE), TILE)
            merged_ref[:, cols] = e_ref[:, cols].astype(F32) + nn(xt_ref[...], gbuf[:, cols])

    def term(shift):
        t = lax.rem(me + shift + n, n)
        at = pl.ds(pl.multiple_of(t * 512, 512), 512)
        return nn(xa[:, slot_cols(shift)], jnp.concatenate([wp[0, at], wp[1, at]], axis=1))

    def product(*shifts):
        yacc[...] += sum(term(shift) for shift in shifts)

    def w_ready(s):
        settle(wp.at[0, pl.ds(0, 1024 if s < 3 else 512)], wc_recv.at[s])

    def piece(j):
        return pl.ds(pl.multiple_of(j * 128, 128), 128)

    my_piece = piece(dp)

    def r_copy(to):
        return pltpu.make_async_remote_copy(
            src_ref=cbuf.at[:, piece(to)], dst_ref=cin.at[dp],
            send_sem=cf_send.at[0], recv_sem=cf_recv.at[0],
            device_id={"dp": to}, device_id_type=MESH)

    def s_copy(k):
        return pltpu.make_async_remote_copy(
            src_ref=coef_ref.at[:, my_piece], dst_ref=coef_ref.at[:, my_piece],
            send_sem=cf_send.at[1], recv_sem=cf_recv.at[1],
            device_id={"dp": d_to[k]}, device_id_type=MESH)

    lc.wait()
    for k in range(1, n):
        c_copy(k).start()
    wz[core, y, xq, pl.ds(pl.multiple_of(me * 8, 8), 8)] = wc_ref[:, pl.ds(pl.multiple_of(dp * 128, 128), 128)]
    lx.wait()
    for k in (1, -1, -2, 2, -3, 3, 4):
        xz_copy(k).start()
    lg.wait()
    g_step(0)
    for c in lw:
        c.wait()
    w_step(0)
    xa[mine, slot_cols(0)] = x_ref[own, :]
    for i in range(n):
        rows = pl.ds(pl.multiple_of(lax.rem(me + SLOTS[i] + n, n) * 32, 32), 32)
        xg_ref[i * 32 : i * 32 + 32, :] = x_ref[rows, :]
    xt_ref[...] = xg_ref[...].T
    settle(wz.at[0, 0, 0, pl.ds(0, 56)], c_recv)
    for h in range(2):
        for k in range(1, 4):
            p_copy(h, 0, k).start()
    settle(xa.at[pl.ds(0, 32), pl.ds(0, 1536)], xz_recv.at[0])
    xy_full(0, 0)
    xy_full(0, 1)
    le.wait()
    se_ref[...] = jnp.zeros_like(se_ref)

    def sketch_error(low, high):
        @pl.loop(low, high, step=TILE)
        def _(c):
            cols = pl.ds(pl.multiple_of(c, TILE), TILE)
            se_ref[...] += nt(split3(wc_ref[:, cols]), e_ref[:, cols])

    sketch_error(0, 2048)
    for h in range(2):
        settle(wz.at[0, 0, pl.ds(0, 3), pl.ds(0, 32)], p_recv.at[h, 0])
        for k in range(1, 4):
            p_copy(h, 1, k).start()
    settle(xa.at[pl.ds(0, 32), pl.ds(0, 2048)], xz_recv.at[1])
    xy_full(1, 0)
    xy_full(1, 1)
    xy_one(0, 0)
    xy_full(0, 2)
    xy_one(0, 1)
    sketch_error(2048, 4096)
    g_step(1)
    for h in range(2):
        settle(wz.at[0, pl.ds(0, 3), :, pl.ds(0, 32)], p_recv.at[h, 1])
        k_copy(h).start()
    settle(wz.at[0], k_recv)
    for d in range(DP):
        w3_ref[:, d * 128 : d * 128 + 128] = split3(wz[d % CORES, d // PLANE, d % PLANE // CORES])
    lp.wait()
    partial = sum3(nt(w3_ref[...], gpad[...]))
    for t in range(n):
        tsrc[t] = partial[t * 8 : t * 8 + 8]
    for k in range(1, n):
        t_copy(k).start()
    tdst[me] = tsrc[me]
    xy_one(1, 0)
    xy_full(1, 2)
    xy_full(0, 3)
    xy_full(1, 3)
    w_step(1)
    xy_two(0, 0)
    xy_one(1, 1)
    g_step(2)
    settle(tdst.at[pl.ds(0, 7)], t_recv)
    tokens = jnp.concatenate(
        [tdst[0] + tdst[1] + tdst[2] + tdst[3], tdst[4] + tdst[5] + tdst[6] + tdst[7]], axis=1)
    sketch = sum3(se_ref[...]) + sum3(nn(split3(tokens), x_ref[...]))
    ks_a, ks_b = range(1, PLANE), range(1, YS)
    sk_src[0] = sketch
    for k in ks_a:
        a_copy(k, sk_src.at[0], abuf.at[xc], sk_send, sk_recv).start()
    abuf[xc] = sketch
    xy_two(1, 0)
    xy_one(0, 2)
    xy_one(1, 2)
    w_step(2)
    settle(abuf.at[pl.ds(0, PLANE - 1)], sk_recv.at[0])
    total = abuf[0]
    for k in range(1, PLANE):
        total += abuf[k]
    sk_src[1] = total
    for k in ks_b:
        b_copy(k, sk_src.at[1], bbuf.at[y], sk_send, sk_recv).start()
    bbuf[y] = total
    g_step(3)
    xy_one(0, 3)
    xy_one(1, 3)
    xy_one(0, 4)
    xy_one(1, 4)
    settle(bbuf.at[pl.ds(0, YS - 1)], sk_recv.at[1])
    total = bbuf[0]
    for k in range(1, YS):
        total += bbuf[k]
    unit = orthonormal(total)
    u_ref[...] = unit
    u3 = split3(unit)
    v3 = split3(sum3(nt(u3, xg_ref[0:224, :])))
    v_last = split3(sum3(nt(u3, xg_ref[224:256, :])))
    w_step(3)

    @pl.loop(0, 4096, step=TILE)
    def _(c):
        cols = pl.ds(pl.multiple_of(c, TILE), TILE)
        cbuf[:, cols] = sum3(nn(u3, e_ref[:, cols]) + nn(v3, gbuf[0:224, cols]))

    g_step(4)

    def coefficients(row):
        cols = pl.ds(pl.multiple_of(row * 1024, 1024), 1024)
        cbuf[:, cols] += sum3(nn(v_last, gbuf[224:256, cols]))

    for dy in (2, 1, 3):
        row = lax.rem(y + dy, YS)
        coefficients(row)
        for j in range(PLANE):
            r_copy(row * PLANE + j).start()
    coefficients(y)
    for k in ks_a:
        r_copy(a_to[k]).start()
    cin[dp] = cbuf[:, my_piece]
    w_step(4)
    for h in range(2):
        for stage in range(1, 5):
            xy_two(h, stage)
    yacc[...] = term(0)
    w_ready(0)
    product(1, -1)
    w_ready(1)
    product(2, -2)
    w_ready(2)
    product(3, -3)
    w_ready(3)
    yb[...] = (yacc[...] + term(4)).astype(BF16)
    for k in range(XS * YS - 1):
        y_copy(k).start()
    out_ref[:, chip_cols] = yb[mine, :]
    settle(cin.at[pl.ds(0, DP - 1)], cf_recv.at[0])
    total = cin[0]
    for k in range(1, DP):
        total += cin[k]
    coef_ref[:, my_piece] = total * (1.0 / 32)
    for k in range(DP - 1):
        s_copy(k).start()
    merge(0, 4096)
    settle(coef_ref.at[:, pl.ds(0, 128 * (DP - 1))], cf_recv.at[1])
    settle(cbuf.at[:, pl.ds(0, 128 * (DP - 1))], cf_send.at[0])
    settle(coef_ref.at[:, pl.ds(0, 128 * (DP - 1))], cf_send.at[1])
    settle(abuf.at[pl.ds(0, PLANE - 1)], sk_send.at[0])
    settle(bbuf.at[pl.ds(0, YS - 1)], sk_send.at[1])
    settle(xa.at[pl.ds(0, 32), pl.ds(0, 3584)], xz_send)
    settle(wz.at[0, 0, 0, pl.ds(0, 56)], c_send)
    settle(tdst.at[pl.ds(0, 7)], t_send)
    settle(wz.at[0], k_send)
    for h in range(2):
        settle(wz.at[0, 0, pl.ds(0, 3), pl.ds(0, 32)], p_send.at[h, 0])
        settle(wz.at[0, pl.ds(0, 3), :, pl.ds(0, 32)], p_send.at[h, 1])
    settle(gbuf.at[pl.ds(0, 224)], g_send)
    settle(wp.at[0, pl.ds(0, 3584)], w_send)
    settle(wp.at[0, pl.ds(0, 3584)], wc_send)
    settle(xa.at[pl.ds(0, 480)], xy_send)
    settle(yb.at[pl.ds(0, 480)], y_recv)
    settle(yb.at[pl.ds(0, 480)], y_send)


def error_kernel(m_ref, u_ref, c_ref, y_ref, o_hbm, out_hbm, coef_hbm, basis_hbm, o_ref, basis_ref, sem, o_sem):
    basis_ref[...] = u_ref[...] * math.sqrt(512)
    through = [pltpu.make_async_copy(a, b, sem.at[i]) for i, (a, b) in enumerate(
        ((y_ref, out_hbm), (c_ref, coef_hbm), (basis_ref, basis_hbm)))]
    for c in through:
        c.start()
    u0, u1, u2 = pieces(u_ref[...])
    left = jnp.concatenate([u0, u0, u1, u0, u2, u1], axis=0).T.astype(BF16)
    width = 4096 // PARTS
    stores = []
    for i in range(PARTS):
        cols = pl.ds(i * width, width)
        c0, c1, c2 = pieces(c_ref[:, cols])
        right = jnp.concatenate([c0, c1, c0, c2, c0, c1], axis=0).astype(BF16)
        for r in range(0, 512, 256):
            for c in range(0, width, 256):
                at = (slice(r, r + 256), pl.ds(i * width + c, 256))
                o_ref[at] = (m_ref[at] - nn(left[r : r + 256], right[:, c : c + 256])).astype(BF16)
        stores.append(pltpu.make_async_copy(o_ref.at[:, cols], o_hbm.at[:, cols], o_sem.at[i]))
        stores[i].start()
    for c in stores + through:
        c.wait()


def shards(inputs, weight, out_grad, error_feedback, warm_coeffs):
    S = jax.ShapeDtypeStruct
    V = pl.BlockSpec(memory_space=pltpu.VMEM)
    A = pl.BlockSpec(memory_space=pl.ANY)
    D = pltpu.SemaphoreType.DMA
    VM = pltpu.VMEM
    hbm = lambda v: pltpu.with_memory_space_constraint(v, pltpu.HBM)
    operands = [hbm(v) for v in (inputs, weight, out_grad, error_feedback[0], warm_coeffs[0])]
    out, coef, merged, unit = pl.pallas_call(
        main_kernel,
        out_shape=(VM((32, 4096), BF16), VM((8, 4096), F32), VM((512, 4096), F32), VM((8, 512), F32)),
        in_specs=[A, A, A, A, A],
        out_specs=(V, V, V, V),
        scratch_shapes=[
            VM((256, 512), BF16),
            VM((512, 4096), BF16),
            VM((256, 4096), BF16),
            VM((512, 4096), BF16),
            VM((CORES, 4096, 128), BF16),
            VM((512, 256), F32),
            VM((512, 256), BF16),
            VM((8, 4096), F32),
            VM((CORES, YS, XS, 64, 128), F32),
            VM((192, 4096), BF16),
            VM((128, 4096), BF16),
            VM((8, 8, 128), F32),
            VM((8, 8, 128), F32),
            VM((24, 512), F32),
            VM((512, 256), BF16),
            VM((256, 512), BF16),
            VM((8, 4096), F32),
            VM((PLANE, 8, 512), F32),
            VM((YS, 8, 512), F32),
            VM((DP, 8, 128), F32),
            VM((2, 8, 512), F32),
            D((7,)),
            D, D((2, 2, 4)),
            D, D((2,)),
            D, D((2, 5, 2)),
            D, D((2, 2, 4)),
            D, D((4,)),
            D, D,
            D((2,)), D((2,)),
            D((2,)), D((2,)),
            D, D,
            D((2, 2)), D((2, 2)),
            D, D,
            D, D,
        ],
        compiler_params=pltpu.CompilerParams(
            collective_id=0, has_side_effects=True, vmem_limit_bytes=40 * 2**20),
    )(*operands)
    err, out, coef, basis = pl.pallas_call(
        error_kernel,
        out_shape=(S((512, 4096), BF16), S((32, 4096), BF16), S((8, 4096), F32), S((8, 512), F32)),
        in_specs=[V, V, V, V],
        out_specs=(A, A, A, A),
        scratch_shapes=[VM((512, 4096), BF16), VM((8, 512), F32), D((3,)), D((PARTS,))],
        compiler_params=pltpu.CompilerParams(vmem_limit_bytes=24 * 2**20),
    )(merged, unit, coef, out)
    return (out, basis, coef[None], err[None])


def solution(mesh):
    in_specs = (
        P("dp", "tensor"),
        P("tensor", None),
        P(("dp", "tensor"), None),
        P("dp", "tensor", None),
        P("tensor", None, None),
    )
    out_specs = (
        P(("dp", "tensor"), None),
        P(None, "tensor"),
        P("tensor", None, None),
        P("dp", "tensor", None),
    )
    return jax.shard_map(shards, mesh=mesh, in_specs=in_specs, out_specs=out_specs, check_vma=False)
```

```python
import functools
import math

import jax
import jax.numpy as jnp
from jax import lax
from jax.experimental import pallas as pl
from jax.experimental.pallas import tpu as pltpu
from jax.sharding import PartitionSpec as P

MESH = pl.DeviceIdType.MESH
F32 = jnp.float32
BF16 = jnp.bfloat16
EPSILON = 1e-06
TILE = 512
PARTS = 8
SLOTS = (0, -1, 1, 2, -2, 3, -3, 4)
XS, YS, CORES = 4, 4, 2
PLANE = XS * CORES
DP = YS * PLANE
OFFSETS = sorted(
    ((dy, dx, dc) for dy in range(YS) for dx in range(XS) for dc in range(CORES)),
    key=lambda o: (-min(o[0], YS - o[0]) - min(o[1], XS - o[1]), -o[2]))


def nn(a, b):
    return lax.dot_general(a, b, (((1,), (0,)), ((), ())), preferred_element_type=F32)


def nt(a, b):
    return lax.dot_general(a, b, (((1,), (1,)), ((), ())), preferred_element_type=F32)


def pieces(v):
    high = v.astype(BF16).astype(F32)
    rest = v - high
    middle = rest.astype(BF16).astype(F32)
    return high, middle, rest - middle


def split3(v):
    return jnp.concatenate(pieces(v), axis=0).astype(BF16)


def sum3(v):
    n = v.shape[0] // 3
    return v[:n] + v[n : 2 * n] + v[2 * n :]


def orthonormal(v):
    rows = lax.broadcasted_iota(jnp.int32, (v.shape[0], 1), 0)
    for i in range(v.shape[0]):
        row = v[i : i + 1]
        dots = jnp.sum(v * row, axis=1, keepdims=True)
        scale = lax.rsqrt(dots[i : i + 1] + EPSILON)
        unit = row * scale
        v = jnp.where(rows == i, unit, jnp.where(rows > i, v - (dots * scale) * unit, v))
    return v


def main_kernel(
    x_hbm, w_hbm, g_hbm, e_hbm, wc_hbm,
    out_ref, coef_ref, merged_ref, u_ref,
    x_ref, e_ref, gbuf, xa, wp, yacc, yb, wc_ref, wz, w3_ref, gpad, tsrc, tdst, se_ref, xt_ref, xg_ref, cbuf,
    abuf, bbuf, cin, sk_src,
    lsem, g_send, g_recv, xz_send, xz_recv, xy_send, xy_recv, w_send, w_recv, wc_send, wc_recv,
    y_send, y_recv, sk_send, sk_recv, cf_send, cf_recv, c_send, c_recv, p_send, p_recv, k_send, k_recv,
    t_send, t_recv,
):
    n = 8
    me = lax.axis_index("tensor")
    dp = lax.axis_index("dp")
    core = dp % CORES
    chip = dp // CORES
    y, xc = dp // PLANE, dp % PLANE
    xq = xc // CORES
    z_all = [lax.rem(me + k, n) for k in range(n)]
    z_to = [z_all[1], z_all[n - 1]]
    sign = (1, -1)
    a_to = [y * PLANE + lax.rem(xc + k, PLANE) for k in range(PLANE)]
    b_to = [lax.rem(y + k, YS) * PLANE + xc for k in range(YS)]
    d_to = [lax.rem(y + dy, YS) * PLANE + lax.rem(xq + dx, XS) * CORES + lax.rem(core + dc, CORES) for dy, dx, dc in OFFSETS]
    chips = [lax.rem(y + dy, YS) * XS + lax.rem(xq + dx, XS) for dy, dx, dc in OFFSETS if dc == 0]
    p_to = [c * CORES + core for c in chips]
    partner = chip * CORES + (1 - core)

    def shifted(axis, r):
        if axis == 0:
            return y * XS + lax.rem(xq + r + XS, XS)
        return lax.rem(y + r + YS, YS) * XS + xq

    own = pl.ds(pl.multiple_of(me * 32, 32), 32)
    mine = pl.ds(pl.multiple_of(chip * 32, 32), 32)
    own_cols = pl.ds(pl.multiple_of(me * 512, 512), 512)
    own_rows = own_cols
    chip_cols = pl.ds(pl.multiple_of(chip * 256, 256), 256)
    lx = pltpu.make_async_copy(x_hbm, x_ref, lsem.at[0])
    lw = [pltpu.make_async_copy(
        w_hbm.at[:, pl.ds(pl.multiple_of(chip * 256 + c * 128, 128), 128)], wp.at[c, own_rows], lsem.at[1 + 5 * c])
        for c in range(CORES)]
    le = pltpu.make_async_copy(e_hbm, e_ref, lsem.at[2])
    lg = pltpu.make_async_copy(g_hbm, gbuf.at[pl.ds(0, 32)], lsem.at[3])
    lc = pltpu.make_async_copy(wc_hbm, wc_ref, lsem.at[5])
    lp = pltpu.make_async_copy(g_hbm, gpad.at[pl.ds(pl.multiple_of(lax.rem(me, 4) * 32, 32), 32)], lsem.at[4])
    for c in (lc, lx, lg, le, *lw):
        c.start()

    barrier = pltpu.get_barrier_semaphore()
    for z in z_all[1:]:
        pl.semaphore_signal(barrier, inc=1, device_id={"tensor": z}, device_id_type=MESH)
    near = [y * PLANE + lax.rem(xq + k, XS) * CORES + core for k in range(1, XS)] + b_to[1:] + [partner]
    for d in near:
        pl.semaphore_signal(barrier, inc=1, device_id={"dp": d}, device_id_type=MESH)
    pl.semaphore_wait(barrier, 7 + 3 + 3 + 1)

    def settle(ref, sem):
        pltpu.make_async_copy(ref, ref, sem).wait()

    def steps(d, h):
        return 4 if d == h else 3

    def ring_copy(buf, rows, part, send, recv, d, h, s):
        block = lax.rem(me - sign[d] * s + n, n)
        at = pl.ds(pl.multiple_of(block * rows + h * part, part), part)
        return pltpu.make_async_remote_copy(
            src_ref=buf.at[at], dst_ref=buf.at[at],
            send_sem=send, recv_sem=recv.at[d, h, s],
            device_id={"tensor": z_to[d]}, device_id_type=MESH)

    def g_copy(d, h, s):
        def at(shift):
            return gbuf.at[pl.ds(SLOTS.index(4 if abs(shift) == 4 else shift) * 32 + h * 16, 16)]

        return pltpu.make_async_remote_copy(
            src_ref=at(-sign[d] * s), dst_ref=at(-sign[d] * (s + 1)),
            send_sem=g_send, recv_sem=g_recv.at[d, h, s],
            device_id={"tensor": z_to[d]}, device_id_type=MESH)

    def w_copy(d, h, s):
        return ring_copy(wp.at[core], 512, 256, w_send, w_recv, d, h, s)

    def wc_copy(d, h, s):
        block = lax.rem(me - sign[d] * (s + 1) + n, n)
        at = pl.ds(pl.multiple_of(block * 512 + h * 256, 256), 256)
        return pltpu.make_async_remote_copy(
            src_ref=wp.at[core, at], dst_ref=wp.at[core, at],
            send_sem=wc_send, recv_sem=wc_recv.at[s],
            device_id={"dp": partner}, device_id_type=MESH)

    def g_step(s):
        for h in range(2):
            for d in range(2):
                if s > 0 and s - 1 < steps(d, h):
                    g_copy(d, h, s - 1).wait_recv()
                if s < steps(d, h):
                    g_copy(d, h, s).start()

    def w_step(s):
        for h in range(2):
            for d in range(2):
                if s > 0 and s - 1 < steps(d, h):
                    w_copy(d, h, s - 1).wait_recv()
                if s < steps(d, h):
                    w_copy(d, h, s).start()
                if s > 0 and s - 1 < steps(d, h):
                    wc_copy(d, h, s - 1).start()

    def slot_cols(shift):
        return pl.ds(SLOTS.index(shift) * 512, 512)

    def xz_copy(k):
        src = pl.ds(pl.multiple_of(lax.rem(me + k + n, n) * 32, 32), 32)
        there = 4 if k == 4 else -k
        return pltpu.make_async_remote_copy(
            src_ref=x_ref.at[src], dst_ref=xa.at[mine, slot_cols(there)],
            send_sem=xz_send, recv_sem=xz_recv.at[SLOTS.index(there) // 4],
            device_id={"tensor": lax.rem(me + k + n, n)}, device_id_type=MESH)

    shifts = (0, -1, 1, 2)

    def xy_copy(h, stage, kind):
        first = h
        second = 1 - h
        axis = first if stage == 0 else second
        r = 0 if stage == 0 else shifts[stage - 1]
        b = (0, 0, -1, 1)[kind]
        go = (1, -1, 1, -1)[kind]
        ra, rb = (b, 0) if stage == 0 else (r, b)
        if first == 0:
            rx, ry = ra, rb
        else:
            rx, ry = rb, ra
        block = lax.rem(y + ry + YS, YS) * XS + lax.rem(xq + rx + XS, XS)
        at = pl.ds(pl.multiple_of(block * 32 + (16 if kind == 3 else 0), 16), 32 if kind < 2 else 16)
        cols = pl.ds(h * 2048, 2048)
        return pltpu.make_async_remote_copy(
            src_ref=xa.at[at, cols], dst_ref=xa.at[at, cols],
            send_sem=xy_send, recv_sem=xy_recv.at[h, stage, kind // 2],
            device_id={"dp": shifted(axis, go) * CORES + core}, device_id_type=MESH)

    def xy_full(h, stage):
        xy_copy(h, stage, 0).start()
        xy_copy(h, stage, 1).start()

    def xy_one(h, stage):
        settle(xa.at[pl.ds(0, 64), pl.ds(0, 2048)], xy_recv.at[h, stage, 0])
        xy_copy(h, stage, 2).start()
        xy_copy(h, stage, 3).start()

    def xy_two(h, stage):
        settle(xa.at[pl.ds(0, 32), pl.ds(0, 2048)], xy_recv.at[h, stage, 1])
        if stage == 0:
            xy_full(h, 4)

    def y_copy(k):
        src = pl.ds(pl.multiple_of(chips[k] * 32, 32), 32)
        return pltpu.make_async_remote_copy(
            src_ref=yb.at[src], dst_ref=out_ref.at[:, chip_cols],
            send_sem=y_send, recv_sem=y_recv,
            device_id={"dp": p_to[k]}, device_id_type=MESH)

    def c_copy(k):
        return pltpu.make_async_remote_copy(
            src_ref=wc_ref.at[:, pl.ds(pl.multiple_of(dp * 128, 128), 128)],
            dst_ref=wz.at[core, y, xq, pl.ds(pl.multiple_of(me * 8, 8), 8)],
            send_sem=c_send, recv_sem=c_recv,
            device_id={"tensor": z_all[k]}, device_id_type=MESH)

    def p_copy(h, phase, k):
        rows = pl.ds(h * 32, 32)
        axis = h if phase == 0 else 1 - h
        if phase == 0:
            at = wz.at[core, y, xq, rows]
        elif axis == 1:
            at = wz.at[core, y, :, rows]
        else:
            at = wz.at[core, :, xq, rows]
        return pltpu.make_async_remote_copy(
            src_ref=at, dst_ref=at, send_sem=p_send.at[h, phase], recv_sem=p_recv.at[h, phase],
            device_id={"dp": shifted(axis, k) * CORES + core}, device_id_type=MESH)

    def k_copy(h):
        at = wz.at[core, :, :, pl.ds(h * 32, 32)]
        return pltpu.make_async_remote_copy(
            src_ref=at, dst_ref=at, send_sem=k_send, recv_sem=k_recv,
            device_id={"dp": partner}, device_id_type=MESH)

    def t_copy(k):
        return pltpu.make_async_remote_copy(
            src_ref=tsrc.at[z_all[k]], dst_ref=tdst.at[me], send_sem=t_send, recv_sem=t_recv,
            device_id={"tensor": z_all[k]}, device_id_type=MESH)

    def a_copy(k, src, dst, send, recv):
        return pltpu.make_async_remote_copy(
            src_ref=src, dst_ref=dst, send_sem=send.at[0], recv_sem=recv.at[0],
            device_id={"dp": a_to[k]}, device_id_type=MESH)

    def b_copy(k, src, dst, send, recv):
        return pltpu.make_async_remote_copy(
            src_ref=src, dst_ref=dst, send_sem=send.at[1], recv_sem=recv.at[1],
            device_id={"dp": b_to[k]}, device_id_type=MESH)

    def merge(low, high):
        @pl.loop(low, high, step=TILE)
        def _(c):
            cols = pl.ds(pl.multiple_of(c, TILE), TILE)
            merged_ref[:, cols] = e_ref[:, cols].astype(F32) + nn(xt_ref[...], gbuf[:, cols])

    def term(shift):
        t = lax.rem(me + shift + n, n)
        at = pl.ds(pl.multiple_of(t * 512, 512), 512)
        return nn(xa[:, slot_cols(shift)], jnp.concatenate([wp[0, at], wp[1, at]], axis=1))

    def product(*shifts):
        yacc[...] += sum(term(shift) for shift in shifts)

    def w_ready(s):
        settle(wp.at[0, pl.ds(0, 1024 if s < 3 else 512)], wc_recv.at[s])

    def piece(j):
        return pl.ds(pl.multiple_of(j * 128, 128), 128)

    my_piece = piece(dp)

    def r_copy(to):
        return pltpu.make_async_remote_copy(
            src_ref=cbuf.at[:, piece(to)], dst_ref=cin.at[dp],
            send_sem=cf_send.at[0], recv_sem=cf_recv.at[0],
            device_id={"dp": to}, device_id_type=MESH)

    def s_copy(k):
        return pltpu.make_async_remote_copy(
            src_ref=coef_ref.at[:, my_piece], dst_ref=coef_ref.at[:, my_piece],
            send_sem=cf_send.at[1], recv_sem=cf_recv.at[1],
            device_id={"dp": d_to[k]}, device_id_type=MESH)

    lc.wait()
    for k in range(1, n):
        c_copy(k).start()
    wz[core, y, xq, pl.ds(pl.multiple_of(me * 8, 8), 8)] = wc_ref[:, pl.ds(pl.multiple_of(dp * 128, 128), 128)]
    lx.wait()
    for k in (1, -1, -2, 2, -3, 3, 4):
        xz_copy(k).start()
    lg.wait()
    g_step(0)
    for c in lw:
        c.wait()
    w_step(0)
    gpad[...] = jnp.zeros_like(gpad)
    lp.start()
    xa[mine, slot_cols(0)] = x_ref[own, :]
    for i in range(n):
        rows = pl.ds(pl.multiple_of(lax.rem(me + SLOTS[i] + n, n) * 32, 32), 32)
        xg_ref[i * 32 : i * 32 + 32, :] = x_ref[rows, :]
    xt_ref[...] = xg_ref[...].T
    settle(wz.at[0, 0, 0, pl.ds(0, 56)], c_recv)
    for h in range(2):
        for k in range(1, 4):
            p_copy(h, 0, k).start()
    settle(xa.at[pl.ds(0, 32), pl.ds(0, 1536)], xz_recv.at[0])
    xy_full(0, 0)
    xy_full(0, 1)
    le.wait()
    se_ref[...] = jnp.zeros_like(se_ref)

    def sketch_error(low, high):
        @pl.loop(low, high, step=TILE)
        def _(c):
            cols = pl.ds(pl.multiple_of(c, TILE), TILE)
            se_ref[...] += nt(split3(wc_ref[:, cols]), e_ref[:, cols])

    sketch_error(0, 2048)
    for h in range(2):
        settle(wz.at[0, 0, pl.ds(0, 3), pl.ds(0, 32)], p_recv.at[h, 0])
        for k in range(1, 4):
            p_copy(h, 1, k).start()
    settle(xa.at[pl.ds(0, 32), pl.ds(0, 2048)], xz_recv.at[1])
    xy_full(1, 0)
    xy_full(1, 1)
    xy_one(0, 0)
    xy_full(0, 2)
    xy_one(0, 1)
    sketch_error(2048, 4096)
    g_step(1)
    for h in range(2):
        settle(wz.at[0, pl.ds(0, 3), :, pl.ds(0, 32)], p_recv.at[h, 1])
        k_copy(h).start()
    settle(wz.at[0], k_recv)
    for d in range(DP):
        w3_ref[:, d * 128 : d * 128 + 128] = split3(wz[d % CORES, d // PLANE, d % PLANE // CORES])
    lp.wait()
    partial = sum3(nt(w3_ref[...], gpad[...]))
    for t in range(n):
        tsrc[t] = partial[t * 8 : t * 8 + 8]
    for k in range(1, n):
        t_copy(k).start()
    tdst[me] = tsrc[me]
    xy_one(1, 0)
    xy_full(1, 2)
    xy_full(0, 3)
    xy_full(1, 3)
    w_step(1)
    xy_two(0, 0)
    xy_one(1, 1)
    g_step(2)
    settle(tdst.at[pl.ds(0, 7)], t_recv)
    tokens = jnp.concatenate(
        [tdst[0] + tdst[1] + tdst[2] + tdst[3], tdst[4] + tdst[5] + tdst[6] + tdst[7]], axis=1)
    sketch = sum3(se_ref[...]) + sum3(nn(split3(tokens), x_ref[...]))
    ks_a, ks_b = range(1, PLANE), range(1, YS)
    sk_src[0] = sketch
    for k in ks_a:
        a_copy(k, sk_src.at[0], abuf.at[xc], sk_send, sk_recv).start()
    abuf[xc] = sketch
    xy_two(1, 0)
    xy_one(0, 2)
    xy_one(1, 2)
    w_step(2)
    settle(abuf.at[pl.ds(0, PLANE - 1)], sk_recv.at[0])
    total = abuf[0]
    for k in range(1, PLANE):
        total += abuf[k]
    sk_src[1] = total
    for k in ks_b:
        b_copy(k, sk_src.at[1], bbuf.at[y], sk_send, sk_recv).start()
    bbuf[y] = total
    g_step(3)
    xy_one(0, 3)
    xy_one(1, 3)
    xy_one(0, 4)
    xy_one(1, 4)
    settle(bbuf.at[pl.ds(0, YS - 1)], sk_recv.at[1])
    total = bbuf[0]
    for k in range(1, YS):
        total += bbuf[k]
    unit = orthonormal(total)
    u_ref[...] = unit
    u3 = split3(unit)
    v3 = split3(sum3(nt(u3, xg_ref[0:224, :])))
    v_last = split3(sum3(nt(u3, xg_ref[224:256, :])))
    w_step(3)

    @pl.loop(0, 4096, step=TILE)
    def _(c):
        cols = pl.ds(pl.multiple_of(c, TILE), TILE)
        cbuf[:, cols] = sum3(nn(u3, e_ref[:, cols]) + nn(v3, gbuf[0:224, cols]))

    g_step(4)

    def coefficients(row):
        cols = pl.ds(pl.multiple_of(row * 1024, 1024), 1024)
        cbuf[:, cols] += sum3(nn(v_last, gbuf[224:256, cols]))

    for dy in (2, 1, 3):
        row = lax.rem(y + dy, YS)
        coefficients(row)
        for j in range(PLANE):
            r_copy(row * PLANE + j).start()
    coefficients(y)
    for k in ks_a:
        r_copy(a_to[k]).start()
    cin[dp] = cbuf[:, my_piece]
    w_step(4)
    for h in range(2):
        for stage in range(1, 5):
            xy_two(h, stage)
    yacc[...] = term(0)
    w_ready(0)
    product(1, -1)
    w_ready(1)
    product(2, -2)
    w_ready(2)
    product(3, -3)
    w_ready(3)
    yb[...] = (yacc[...] + term(4)).astype(BF16)
    for k in range(XS * YS - 1):
        y_copy(k).start()
    out_ref[:, chip_cols] = yb[mine, :]
    settle(cin.at[pl.ds(0, DP - 1)], cf_recv.at[0])
    total = cin[0]
    for k in range(1, DP):
        total += cin[k]
    coef_ref[:, my_piece] = total * (1.0 / 32)
    for k in range(DP - 1):
        s_copy(k).start()
    merge(0, 4096)
    settle(coef_ref.at[:, pl.ds(0, 128 * (DP - 1))], cf_recv.at[1])
    settle(cbuf.at[:, pl.ds(0, 128 * (DP - 1))], cf_send.at[0])
    settle(coef_ref.at[:, pl.ds(0, 128 * (DP - 1))], cf_send.at[1])
    settle(abuf.at[pl.ds(0, PLANE - 1)], sk_send.at[0])
    settle(bbuf.at[pl.ds(0, YS - 1)], sk_send.at[1])
    settle(xa.at[pl.ds(0, 32), pl.ds(0, 3584)], xz_send)
    settle(wz.at[0, 0, 0, pl.ds(0, 56)], c_send)
    settle(tdst.at[pl.ds(0, 7)], t_send)
    settle(wz.at[0], k_send)
    for h in range(2):
        settle(wz.at[0, 0, pl.ds(0, 3), pl.ds(0, 32)], p_send.at[h, 0])
        settle(wz.at[0, pl.ds(0, 3), :, pl.ds(0, 32)], p_send.at[h, 1])
    settle(gbuf.at[pl.ds(0, 224)], g_send)
    settle(wp.at[0, pl.ds(0, 3584)], w_send)
    settle(wp.at[0, pl.ds(0, 3584)], wc_send)
    settle(xa.at[pl.ds(0, 480)], xy_send)
    settle(yb.at[pl.ds(0, 480)], y_recv)
    settle(yb.at[pl.ds(0, 480)], y_send)


def error_kernel(m_ref, u_ref, c_ref, y_ref, o_hbm, out_hbm, coef_hbm, basis_hbm, o_ref, basis_ref, sem, o_sem):
    basis_ref[...] = u_ref[...] * math.sqrt(512)
    through = [pltpu.make_async_copy(a, b, sem.at[i]) for i, (a, b) in enumerate(
        ((y_ref, out_hbm), (c_ref, coef_hbm), (basis_ref, basis_hbm)))]
    for c in through:
        c.start()
    u0, u1, u2 = pieces(u_ref[...])
    left = jnp.concatenate([u0, u0, u1, u0, u2, u1], axis=0).T.astype(BF16)
    width = 4096 // PARTS
    stores = []
    for i in range(PARTS):
        cols = pl.ds(i * width, width)
        c0, c1, c2 = pieces(c_ref[:, cols])
        right = jnp.concatenate([c0, c1, c0, c2, c0, c1], axis=0).astype(BF16)
        for r in range(0, 512, 256):
            for c in range(0, width, 256):
                at = (slice(r, r + 256), pl.ds(i * width + c, 256))
                o_ref[at] = (m_ref[at] - nn(left[r : r + 256], right[:, c : c + 256])).astype(BF16)
        stores.append(pltpu.make_async_copy(o_ref.at[:, cols], o_hbm.at[:, cols], o_sem.at[i]))
        stores[i].start()
    for c in stores + through:
        c.wait()


def shards(inputs, weight, out_grad, error_feedback, warm_coeffs):
    S = jax.ShapeDtypeStruct
    V = pl.BlockSpec(memory_space=pltpu.VMEM)
    A = pl.BlockSpec(memory_space=pl.ANY)
    D = pltpu.SemaphoreType.DMA
    VM = pltpu.VMEM
    hbm = lambda v: pltpu.with_memory_space_constraint(v, pltpu.HBM)
    operands = [hbm(v) for v in (inputs, weight, out_grad, error_feedback[0], warm_coeffs[0])]
    out, coef, merged, unit = pl.pallas_call(
        main_kernel,
        out_shape=(VM((32, 4096), BF16), VM((8, 4096), F32), VM((512, 4096), F32), VM((8, 512), F32)),
        in_specs=[A, A, A, A, A],
        out_specs=(V, V, V, V),
        scratch_shapes=[
            VM((256, 512), BF16),
            VM((512, 4096), BF16),
            VM((256, 4096), BF16),
            VM((512, 4096), BF16),
            VM((CORES, 4096, 128), BF16),
            VM((512, 256), F32),
            VM((512, 256), BF16),
            VM((8, 4096), F32),
            VM((CORES, YS, XS, 64, 128), F32),
            VM((192, 4096), BF16),
            VM((128, 4096), BF16),
            VM((8, 8, 128), F32),
            VM((8, 8, 128), F32),
            VM((24, 512), F32),
            VM((512, 256), BF16),
            VM((256, 512), BF16),
            VM((8, 4096), F32),
            VM((PLANE, 8, 512), F32),
            VM((YS, 8, 512), F32),
            VM((DP, 8, 128), F32),
            VM((2, 8, 512), F32),
            D((7,)),
            D, D((2, 2, 4)),
            D, D((2,)),
            D, D((2, 5, 2)),
            D, D((2, 2, 4)),
            D, D((4,)),
            D, D,
            D((2,)), D((2,)),
            D((2,)), D((2,)),
            D, D,
            D((2, 2)), D((2, 2)),
            D, D,
            D, D,
        ],
        compiler_params=pltpu.CompilerParams(
            collective_id=0, has_side_effects=True, vmem_limit_bytes=40 * 2**20),
    )(*operands)
    err, out, coef, basis = pl.pallas_call(
        error_kernel,
        out_shape=(S((512, 4096), BF16), S((32, 4096), BF16), S((8, 4096), F32), S((8, 512), F32)),
        in_specs=[V, V, V, V],
        out_specs=(A, A, A, A),
        scratch_shapes=[VM((512, 4096), BF16), VM((8, 512), F32), D((3,)), D((PARTS,))],
        compiler_params=pltpu.CompilerParams(vmem_limit_bytes=24 * 2**20),
    )(merged, unit, coef, out)
    return (out, basis, coef[None], err[None])


def solution(mesh):
    in_specs = (
        P("dp", "tensor"),
        P("tensor", None),
        P(("dp", "tensor"), None),
        P("dp", "tensor", None),
        P("tensor", None, None),
    )
    out_specs = (
        P(("dp", "tensor"), None),
        P(None, "tensor"),
        P("tensor", None, None),
        P("dp", "tensor", None),
    )
    return jax.shard_map(shards, mesh=mesh, in_specs=in_specs, out_specs=out_specs, check_vma=False)
```
